32 devices in a mesh: ctx: 8 (over z, y), head: 4 (over x, core).
Axes of the slice: x: 2, y: 2, z: 4, core: 2. Of those that a mesh axis runs over, the one named last changes fastest.
Arguments:
- ctx_queries: bfloat16 [8192, 4096], P('ctx', 'head'), may hold values from -8 to 8
- ctx_keys: bfloat16 [8192, 512], P('ctx', 'head'), may hold values from -12 to 12
- ctx_values: bfloat16 [8192, 512], P('ctx', 'head'), may hold values from -12 to 12
- new_queries: bfloat16 [64, 4096], P('ctx', 'head'), may hold values from -8 to 8
- out_weight: bfloat16 [4096, 8192], P('head', 'ctx'), may hold values from -0.09375 to 0.09375
- host_block: int32 [8], replicated, may hold values from 0 to 7, each once
- block_lengths: int32 [8], replicated, may hold values from 256 to 1024, as said below
Outputs:
- context_out: bfloat16 [8192, 4096], P('ctx', 'head')
- answer: bfloat16 [64, 8192], P('head', 'ctx')
The draws below stay inside these ranges and needn't reach their ends.
Inputs may be any that keep to these rules, and one draw needn't show every extreme that they name: `block_lengths`: some block has 1024 valid tokens and another exactly 256. `host_block`: a permutation of the blocks.
All inputs are finite; a program needn't handle non-finite values.
Results may differ from the reference program's by a relative error of at most 0.002.
The reference program's roundings to bfloat16 on the way count: a program that leaves them out, or rounds other values in their place, can miss the bound.
Values may be sent and summed in bfloat16 or wider, within the bound.
No kernel may reach another device: no remote copies, remote signals or barrier semaphores. Data moves between devices by JAX's collectives and lax.ppermute only.
A program may use at most 128 MiB of HBM per device.

```python
import jax
import jax.numpy as jnp
from jax import lax

HD = 128
GROUP = 8
MODEL = 8192
KVH = 4
QH = 32
BLOCK = 1024
NBLK = 8
CTX = 8192
QTOK = 64


def channel_scale(key):
    head_keys = jax.random.split(key, KVH)

    def single_order(single_key):
        return jax.random.permutation(single_key, HD)
    orders = jax.vmap(single_order)(head_keys)
    return jnp.where(orders < 4, 5.0, 1.0).astype(jnp.float32)


def draw_ctx_keys(key, part):
    key = jax.random.fold_in(key, 11)
    scales = channel_scale(jax.random.fold_in(key, 23))
    matrix = jnp.clip(jax.random.normal(key, (NBLK, BLOCK, KVH, HD), jnp.float32), -6.0, 6.0)
    matrix = jnp.clip(matrix * scales[None, None], -12.0, 12.0)
    return matrix.reshape(CTX, KVH * HD).astype(jnp.bfloat16)


def draw_ctx_values(key, part):
    key = jax.random.fold_in(key, 19)
    scales = channel_scale(jax.random.fold_in(key, 29))
    matrix = jnp.clip(jax.random.normal(key, (CTX, KVH, HD), jnp.float32), -6.0, 6.0)
    matrix = jnp.clip(matrix * scales[None], -12.0, 12.0)
    return matrix.reshape(CTX, KVH * HD).astype(jnp.bfloat16)


def draw_ctx_queries(key, part):
    key = jax.random.fold_in(key, 13)
    matrix = jnp.clip(jax.random.normal(key, (NBLK, BLOCK, KVH, GROUP, HD), jnp.float32), -6.0, 6.0)
    coins = jax.random.bernoulli(jax.random.fold_in(key, 31), 0.5, (NBLK, 2, KVH, GROUP, HD))
    levels = jnp.array([8.0, 6.0], jnp.float32)[None, :, None, None, None]
    loud = jnp.where(coins, 1.0, -1.0).astype(jnp.float32) * levels
    matrix = matrix.at[:, 6:8].set(loud)
    return matrix.reshape(CTX, KVH * GROUP * HD).astype(jnp.bfloat16)


def draw_new_queries(key, part):
    key = jax.random.fold_in(key, 17)
    residue = jnp.arange(QTOK, dtype=jnp.int32) % 8
    matrix = jnp.clip(jax.random.normal(key, (QTOK, KVH, GROUP, HD), jnp.float32), -6.0, 6.0)
    coins = jax.random.bernoulli(jax.random.fold_in(key, 41), 0.5, (QTOK, KVH, GROUP, HD))
    level = jnp.where(residue == 4, 8.0, 6.0).astype(jnp.float32)
    loud = jnp.where(coins, 1.0, -1.0).astype(jnp.float32) * level[:, None, None, None]
    chosen_rows = jnp.logical_or(residue == 4, residue == 5)
    matrix = jnp.where(chosen_rows[:, None, None, None], loud, matrix)
    return matrix.reshape(QTOK, KVH * GROUP * HD).astype(jnp.bfloat16)


def draw_block_lengths(key, part):
    key = jax.random.fold_in(key, 5)
    first_key, second_key = jax.random.split(key)
    lengths = jax.random.randint(first_key, (NBLK,), BLOCK // 4, BLOCK + 1)
    chosen = jax.random.randint(second_key, (), 0, NBLK)
    positions = jnp.arange(NBLK, dtype=jnp.int32)
    lengths = jnp.where(positions == chosen, BLOCK, lengths)
    lengths = jnp.where(positions == (chosen + 1) % NBLK, BLOCK // 4, lengths)
    return lengths.astype(jnp.int32)


def block_levels(key, extent, shards, least, high):
    def one(axis_at, parts):
        steps = jax.random.uniform(jax.random.fold_in(jax.random.fold_in(key, 6), axis_at), (parts,), jnp.float32, least / len(shards), high / len(shards))
        return jnp.repeat(jnp.exp(steps), extent[axis_at] // parts).reshape((-1,) + (1,) * (len(extent) - axis_at - 1))

    factor_of = one(*shards[0])
    for cut in shards[1:]:
        factor_of = factor_of * one(*cut)
    return factor_of


def noise(rng, dims, scale, reach, cuts=(), held_as=jnp.bfloat16):
    drawn = scale * jax.random.normal(rng, dims, jnp.float32)
    if cuts:
        drawn = drawn * block_levels(rng, dims, cuts, -0.22, 0.18)
    return jnp.clip(drawn, -reach, reach).astype(held_as)


def setup_inputs(seed: int = 0) -> dict:
    splits = jax.random.split(jax.random.key(seed), 8)
    return {
        "ctx_queries": draw_ctx_queries(jax.random.fold_in(splits[7], 71), 0),
        "ctx_keys": draw_ctx_keys(jax.random.fold_in(splits[7], 71), 0),
        "ctx_values": draw_ctx_values(jax.random.fold_in(splits[7], 71), 0),
        "new_queries": draw_new_queries(jax.random.fold_in(splits[7], 71), 0),
        "out_weight": noise(splits[4], (QH * HD, MODEL), (QH * HD) ** -0.5, 0.09375, ((0, 4), (1, 8))),
        "host_block": jax.random.permutation(splits[5], NBLK).astype(jnp.int32),
        "block_lengths": draw_block_lengths(jax.random.fold_in(splits[7], 71), 0),
    }


NEG = -1e+30
CLIP_FACTOR = 2.0

def sign_matrix(size):
    positions = jnp.arange(size, dtype=jnp.int32)
    common = jnp.bitwise_and(positions[:, None], positions[None, :])
    parity = jnp.zeros((size, size), jnp.int32)
    for bit_number in range(int(size).bit_length()):
        parity = parity + jnp.bitwise_and(jnp.right_shift(common, bit_number), 1)
    parity = parity % 2
    return (1 - 2 * parity).astype(jnp.bfloat16)

def rotate(matrix, sign_table):
    head_width = matrix.shape[-1]
    return (jnp.dot(matrix, sign_table, preferred_element_type=jnp.float32) * head_width ** (-0.5)).astype(jnp.bfloat16)

def store_rotated(matrix, sign_table):
    head_width = matrix.shape[-1]
    turned = jnp.dot(matrix, sign_table, preferred_element_type=jnp.float32) * head_width ** (-0.5)
    ceiling = CLIP_FACTOR * jnp.sqrt(lax.optimization_barrier(jnp.mean(turned * turned, axis=-1, keepdims=True)))
    return jnp.clip(turned, -ceiling, ceiling).astype(jnp.bfloat16)

def block_attention(queries, own_keys, own_values, anchor_keys, anchor_values, own_len, anchor_len, is_anchor):
    row_count = queries.shape[1]
    head_width = queries.shape[2]
    positions = jnp.arange(row_count, dtype=jnp.int32)
    anchor_ok = jnp.logical_and(positions < anchor_len, jnp.logical_not(is_anchor))
    own_ok = jnp.logical_and(positions[None, :] <= positions[:, None], positions[None, :] < own_len)
    allowed = jnp.concatenate([jnp.broadcast_to(anchor_ok[None, :], (row_count, row_count)), own_ok], axis=1)
    all_keys = jnp.concatenate([anchor_keys, own_keys], axis=0)
    all_values = jnp.concatenate([anchor_values, own_values], axis=0)

    def single_head(query_rows):
        scores = jnp.dot(query_rows, all_keys.T, preferred_element_type=jnp.float32) * head_width ** (-0.5)
        scores = jnp.where(allowed, scores, NEG)
        row_max = lax.optimization_barrier(jnp.max(scores, axis=1, keepdims=True))
        powers = jnp.where(allowed, jnp.exp(scores - row_max), 0.0)
        weights = powers.astype(jnp.bfloat16)
        totals = lax.optimization_barrier(jnp.sum(powers, axis=1))
        output = jnp.dot(weights, all_values, preferred_element_type=jnp.float32) / totals[:, None]
        return jnp.where((positions < own_len)[:, None], output, 0.0).astype(jnp.bfloat16)
    return lax.map(single_head, queries)

def host_partial(queries, rot_keys, rot_values, own_len):
    head_width = queries.shape[2]
    usable = jnp.arange(rot_keys.shape[0], dtype=jnp.int32) < own_len

    def single_head(query_rows):
        scores = jnp.dot(query_rows, rot_keys.T, preferred_element_type=jnp.float32) * head_width ** (-0.5)
        scores = jnp.where(usable[None, :], scores, NEG)
        row_max = lax.optimization_barrier(jnp.max(scores, axis=1))
        powers = jnp.where(usable[None, :], jnp.exp(scores - row_max[:, None]), 0.0)
        weights = powers.astype(jnp.bfloat16)
        return (row_max, lax.optimization_barrier(jnp.sum(powers, axis=1)), jnp.dot(weights, rot_values, preferred_element_type=jnp.float32))
    return lax.map(single_head, queries)

def finish(output, totals, sign_table):
    head_width = output.shape[2]
    scaled = output / totals[..., None]
    turned = jnp.einsum('hrd,de->rhe', scaled, sign_table.astype(jnp.float32), precision=lax.Precision.HIGHEST)
    turned = turned * head_width ** (-0.5)
    return turned.reshape(output.shape[1], -1).astype(jnp.bfloat16)

def reference(ctx_queries, ctx_keys, ctx_values, new_queries, out_weight, host_block, block_lengths):
    sign_table = sign_matrix(HD)
    host_ids = jnp.arange(NBLK, dtype=jnp.int32)
    host_len = block_lengths[host_block]
    anchor_host = jnp.sum(jnp.where(host_block == 0, host_ids, 0)).astype(jnp.int32)
    anchor_len = block_lengths[0]
    query_table = ctx_queries.reshape(NBLK, BLOCK, KVH, GROUP, HD)
    key_table = ctx_keys.reshape(NBLK, BLOCK, KVH, HD)
    value_table = ctx_values.reshape(NBLK, BLOCK, KVH, HD)

    def per_host(host_index):
        query_rows = query_table[host_index]
        key_rows = key_table[host_index]
        value_rows = value_table[host_index]
        anchor_k = key_table[anchor_host]
        anchor_v = value_table[anchor_host]

        def each_group(group_index):
            return block_attention(query_rows[:, group_index].transpose(1, 0, 2), key_rows[:, group_index], value_rows[:, group_index], anchor_k[:, group_index], anchor_v[:, group_index], host_len[host_index], anchor_len, host_block[host_index] == 0)
        outputs = lax.map(each_group, jnp.arange(KVH, dtype=jnp.int32))
        return outputs.transpose(2, 0, 1, 3).reshape(BLOCK, QH * HD)
    context_out = lax.map(per_host, host_ids).reshape(CTX, QH * HD)
    query_grid = new_queries.reshape(QTOK, KVH, GROUP, HD)

    def each_group_query(group_index):
        query_rot = rotate(query_grid[:, group_index].reshape(QTOK * GROUP, HD), sign_table)
        query_rot = query_rot.reshape(QTOK, GROUP, HD).transpose(1, 0, 2)

        def per_host_query(host_index):
            key_store = store_rotated(key_table[host_index][:, group_index], sign_table)
            value_store = store_rotated(value_table[host_index][:, group_index], sign_table)
            return host_partial(query_rot, key_store, value_store, host_len[host_index])
        maxima, sums, outputs = lax.map(per_host_query, host_ids)
        overall = lax.optimization_barrier(jnp.max(maxima, axis=0))
        factor = jnp.exp(maxima - overall)
        totals = lax.optimization_barrier(jnp.sum(sums * factor, axis=0))
        output = lax.optimization_barrier(jnp.sum(outputs * factor[..., None], axis=0))
        return finish(output, totals, sign_table)
    pieces = lax.map(each_group_query, jnp.arange(KVH, dtype=jnp.int32))
    attended = pieces.transpose(1, 0, 2).reshape(QTOK, QH * HD)
    answer = jnp.dot(attended, out_weight, preferred_element_type=jnp.float32).astype(jnp.bfloat16)
    return (context_out, answer)
```

```python
import functools

import jax
import jax.numpy as jnp
from jax import lax
from jax.experimental import pallas as pl
from jax.experimental.pallas import tpu as pltpu
from jax.sharding import PartitionSpec as P

HD = 128
CLIP_FACTOR = 2.0
NEG = -1e30
LOG2E = 1.4426950408889634
NT = (((1,), (1,)), ((), ()))
SPREAD = 4
SPREAD_BITS = (1, 2)
TAIL = 8
F32 = jnp.float32
BF16 = jnp.bfloat16


def sign_table(size):
    a = lax.broadcasted_iota(jnp.int32, (size, size), 0)
    b = lax.broadcasted_iota(jnp.int32, (size, size), 1)
    x = jnp.bitwise_and(a, b)
    parity = jnp.zeros((size, size), jnp.int32)
    for bit in range(int(size).bit_length()):
        parity = jnp.bitwise_xor(parity, jnp.bitwise_and(jnp.right_shift(x, bit), 1))
    return (1 - 2 * parity).astype(F32)


def context_kernel(lens, q_ref, k_ref, v_ref, ak_ref, av_ref, o_ref, *, tq, tk, hp, st):
    own_len, anchor_len, anchor_tiles = lens[0], lens[1], lens[2]
    rows, hd = k_ref.shape
    c = hd**-0.5 * LOG2E

    def scores(na, h, i):
        q = [q_ref[i * tq : (i + 1) * tq, (h + e) * hd : (h + e + 1) * hd] for e in range(st)]
        q = jnp.concatenate(q, axis=0)
        parts = []
        if na:
            edge = (na - 1) * tk
            sa = lax.dot_general(q, ak_ref[: na * tk], NT, preferred_element_type=F32)
            col = lax.broadcasted_iota(jnp.int32, (1, tk), 1)
            if na > 1:
                parts.append((sa[:, :edge], av_ref, 0))
            parts.append((jnp.where(col < anchor_len - edge, sa[:, edge:], NEG), av_ref, edge))
        so = lax.dot_general(q, k_ref[: (i + 1) * tq], NT, preferred_element_type=F32)
        r0 = lax.broadcasted_iota(jnp.int32, (tq, tq), 0)
        c0 = lax.broadcasted_iota(jnp.int32, (tq, tq), 1)
        seen = c0 <= r0
        d = [jnp.where(seen, so[e * tq : (e + 1) * tq, i * tq :], NEG) for e in range(st)]
        if i:
            parts.append((so[:, : i * tq], v_ref, 0))
        parts.append((jnp.concatenate(d, axis=0), v_ref, i * tq))
        return parts

    def fold(op, xs):
        return functools.reduce(
            op, [x[:, a : a + 128] for x in xs for a in range(0, x.shape[1], 128)]
        )

    def finish(parts, h, i):
        m = jnp.max(fold(jnp.maximum, [p for p, _, _ in parts]), axis=1, keepdims=True)
        acc = 0.0
        powers = []
        for p, src, at in parts:
            e = jnp.exp2((p - m) * c)
            powers.append(e)
            acc = acc + jnp.dot(
                e.astype(BF16), src[at : at + p.shape[1]], preferred_element_type=F32
            )
        total = jnp.sum(fold(jnp.add, powers), axis=1, keepdims=True)
        row = lax.broadcasted_iota(jnp.int32, (tq, 1), 0) + i * tq
        for e in range(st):
            part = slice(e * tq, (e + 1) * tq)
            out = jnp.where(row < own_len, acc[part] / total[part], 0.0)
            o_ref[i * tq : (i + 1) * tq, (h + e) * hd : (h + e + 1) * hd] = out.astype(BF16)

    def body(na):
        pending = None
        for h in range(0, hp, st):
            for i in range(rows // tq):
                s = scores(na, h, i)
                if pending is not None:
                    finish(*pending)
                pending = (s, h, i)
        finish(*pending)

    for na in range(rows // tk + 1):
        pl.when(anchor_tiles == na)(functools.partial(body, na))


def context_attention(lens, q, k, v, ak, av, tq=128, tk=256, hp=4, st=4):
    rows, width = q.shape
    hd = k.shape[1]
    heads = width // hd
    full = pl.BlockSpec((rows, hd), lambda h, *_: (0, 0))
    wide = pl.BlockSpec((rows, hp * hd), lambda h, *_: (0, h))
    return pl.pallas_call(
        functools.partial(context_kernel, tq=tq, tk=tk, hp=hp, st=st),
        grid_spec=pltpu.PrefetchScalarGridSpec(
            num_scalar_prefetch=1,
            grid=(heads // hp,),
            in_specs=[wide, full, full, full, full],
            out_specs=wide,
        ),
        out_shape=jax.ShapeDtypeStruct(q.shape, q.dtype),
        compiler_params=pltpu.CompilerParams(vmem_limit_bytes=40 << 20),
        cost_estimate=pl.CostEstimate(
            flops=24 * heads * rows * rows * hd // 4,
            bytes_accessed=4 * rows * width + 8 * rows * hd,
            transcendentals=heads * rows * rows * 3 // 2,
        ),
        name="context_attention",
    )(lens, q, k, v, ak, av)


def partial_kernel(scal, *refs, hd, step, blocks):
    q_refs, (k_ref, v_ref), outs, (q_all,) = (
        refs[:SPREAD],
        refs[SPREAD : SPREAD + 2],
        refs[SPREAD + 2 : -1],
        refs[-1:],
    )
    spot, own_len = scal[0], scal[1]
    tokens, width = q_all.shape
    per = width // hd // SPREAD
    scale = hd**-0.5
    table = sign_table(hd)
    table16 = table.astype(BF16)
    for k in range(SPREAD):
        for x in range(blocks):
            at = pl.multiple_of((x * SPREAD + jnp.bitwise_xor(spot, k)) * step, step)
            q_all[pl.ds(at, step), :] = q_refs[k][x * step : (x + 1) * step, :]

    def store(ref):
        r = jnp.dot(ref[...], table16, preferred_element_type=F32) * scale
        ceiling = CLIP_FACTOR * jnp.sqrt(jnp.mean(r * r, axis=-1, keepdims=True))
        return jnp.clip(r, -ceiling, ceiling)

    key_store = store(k_ref).astype(BF16)
    value_turned = store(v_ref).T.astype(BF16)
    rows = k_ref.shape[0]
    usable = lax.broadcasted_iota(jnp.int32, (rows, 1), 0) < own_len
    for k in range(SPREAD):
        at = pl.multiple_of(jnp.bitwise_xor(spot, k) * (per * hd), per * hd)
        q = q_all[:, pl.ds(at, per * hd)]
        q = jnp.concatenate([q[:, e * hd : (e + 1) * hd] for e in range(per)], axis=0)
        rot = (jnp.dot(q, table16, preferred_element_type=F32) * scale).astype(BF16)
        s = lax.dot_general(key_store, rot, NT, preferred_element_type=F32) * scale
        s = jnp.where(usable, s, NEG)
        m = jnp.max(s, axis=0, keepdims=True)
        p = jnp.exp(s - m)
        total = jnp.sum(p, axis=0, keepdims=True)
        outs[k][:hd, :] = jnp.dot(value_turned, p.astype(BF16), preferred_element_type=F32)
        outs[k][hd : hd + 1, :] = m
        outs[k][hd + 1 : hd + 2, :] = total
        outs[k][hd + 2 :, :] = jnp.zeros((TAIL - 2, q.shape[0]), F32)


def host_partials(spot, own_len, pieces, keys, values, heads):
    hd = keys.shape[1]
    width = pieces[0].shape[1]
    tokens = SPREAD * pieces[0].shape[0]
    blocks = pieces[0].shape[0] // 16
    shape = jax.ShapeDtypeStruct((hd + TAIL, tokens * heads // SPREAD), F32)
    whole = pl.BlockSpec(memory_space=pltpu.VMEM)
    return pl.pallas_call(
        functools.partial(partial_kernel, hd=hd, step=16, blocks=blocks),
        in_specs=[pl.BlockSpec(memory_space=pltpu.SMEM)] + [whole] * (SPREAD + 2),
        out_specs=[whole] * SPREAD,
        out_shape=[shape] * SPREAD,
        scratch_shapes=[pltpu.VMEM((tokens, width), BF16)],
        compiler_params=pltpu.CompilerParams(vmem_limit_bytes=24 << 20),
        name="host_partials",
    )(jnp.stack([spot, own_len]), *pieces, keys, values)


def merge_values(parts, hd):
    maxima = [p[hd : hd + 1, :] for p in parts]
    overall = functools.reduce(jnp.maximum, maxima)
    factors = [jnp.exp(m - overall) for m in maxima]
    out = sum(p[:hd, :] * f for p, f in zip(parts, factors))
    total = sum(p[hd + 1 : hd + 2, :] * f for p, f in zip(parts, factors))
    return overall, total, out


def merge_kernel(*refs, hd):
    o_ref = refs[-1]
    overall, total, out = merge_values(refs[:-1], hd)
    o_ref[:hd, :] = out
    o_ref[hd : hd + 1, :] = overall
    o_ref[hd + 1 : hd + 2, :] = total
    o_ref[hd + 2 :, :] = jnp.zeros((TAIL - 2, out.shape[1]), F32)


def merged(parts, hd):
    whole = pl.BlockSpec(memory_space=pltpu.VMEM)
    return pl.pallas_call(
        functools.partial(merge_kernel, hd=hd),
        in_specs=[whole] * len(parts),
        out_specs=whole,
        out_shape=jax.ShapeDtypeStruct(parts[0].shape, F32),
        name="merge_partials",
    )(*parts)


def finish_kernel(*refs, hd, tokens):
    o_ref = refs[-1]
    _, total, out = merge_values(refs[:-1], hd)
    turned = jnp.dot(
        sign_table(hd),
        out / total,
        preferred_element_type=F32,
        precision=lax.Precision.HIGHEST,
    )
    turned = (turned * hd**-0.5).T
    for e in range(turned.shape[0] // tokens):
        o_ref[:, e * hd : (e + 1) * hd] = turned[e * tokens : (e + 1) * tokens].astype(BF16)


def finished(parts, hd, tokens):
    whole = pl.BlockSpec(memory_space=pltpu.VMEM)
    per = parts[0].shape[1] // tokens
    return pl.pallas_call(
        functools.partial(finish_kernel, hd=hd, tokens=tokens),
        in_specs=[whole] * len(parts),
        out_specs=whole,
        out_shape=jax.ShapeDtypeStruct((tokens, per * hd), BF16),
        name="finish_queries",
    )(*parts)


def project_kernel(scal, *refs, groups):
    a_refs, w_ref, outs, total = refs[:SPREAD], refs[SPREAD], refs[SPREAD + 1 : -1], refs[-1]
    spot, head = scal[0], scal[1]
    depth = a_refs[0].shape[1]
    acc = 0.0
    for k in range(SPREAD):
        at = pl.multiple_of(jnp.bitwise_xor(spot, k) * depth, depth)
        acc = acc + jnp.dot(a_refs[k][...], w_ref[pl.ds(at, depth), :], preferred_element_type=F32)
    total[...] = acc
    rows = total.shape[0] // groups
    for k in range(groups):
        at = pl.multiple_of(jnp.bitwise_xor(head, k) * rows, rows)
        outs[k][...] = total[pl.ds(at, rows), :]


def projected(spot, head, chunks, weight, groups):
    tokens = chunks[0].shape[0]
    columns = weight.shape[1]
    whole = pl.BlockSpec(memory_space=pltpu.VMEM)
    return pl.pallas_call(
        functools.partial(project_kernel, groups=groups),
        in_specs=[pl.BlockSpec(memory_space=pltpu.SMEM)] + [whole] * (SPREAD + 1),
        out_specs=[whole] * groups,
        out_shape=[jax.ShapeDtypeStruct((tokens // groups, columns), F32)] * groups,
        scratch_shapes=[pltpu.VMEM((tokens, columns), F32)],
        compiler_params=pltpu.CompilerParams(vmem_limit_bytes=16 << 20),
        name="project",
    )(jnp.stack([spot, head]), *chunks, weight)


def swap(x, axis, flip):
    size = lax.axis_size(axis)
    return lax.ppermute(x, axis, [(i, i ^ flip) for i in range(size)])


def per_device(
    ctx_queries, ctx_keys, ctx_values, new_queries, out_weight, host_block, block_lengths
):
    hosts = lax.axis_size("ctx")
    groups = lax.axis_size("head")
    bits = hosts.bit_length() - 1
    other_bits = [b for b in range(bits) if b not in SPREAD_BITS]
    heads = ctx_queries.shape[1] // HD
    tokens = new_queries.shape[0] * hosts
    me = lax.axis_index("ctx").astype(jnp.int32)
    head = lax.axis_index("head").astype(jnp.int32)
    spot = jnp.bitwise_and(jnp.right_shift(me, 1), SPREAD - 1)

    host_ids = jnp.arange(hosts, dtype=jnp.int32)
    own_block = jnp.sum(jnp.where(host_ids == me, host_block, 0))
    own_len = jnp.sum(jnp.where(host_ids == own_block, block_lengths, 0))
    root = jnp.sum(jnp.where(host_block == 0, host_ids, 0))
    anchor_len = block_lengths[0]
    is_anchor = own_block == 0

    def bit(value, b):
        return jnp.bitwise_and(jnp.right_shift(value, b), 1)

    piece = new_queries
    for b in other_bits:
        got = swap(piece, "ctx", 1 << b)
        low = bit(me, b) == 0
        piece = jnp.concatenate([jnp.where(low, piece, got), jnp.where(low, got, piece)], axis=0)
    pieces = [piece] + [swap(piece, "ctx", k << 1) for k in range(1, SPREAD)]

    even = bit(me, 0) == 0
    held = jnp.where(even, ctx_keys, ctx_values)
    got = swap(jnp.where(even, ctx_values, ctx_keys), "ctx", 1)
    held = jnp.where(bit(root, 0) == bit(me, 0), held, got)
    for b in range(1, bits):
        got = swap(held, "ctx", 1 << b)
        held = jnp.where(bit(root, b) == bit(me, b), held, got)
    got = swap(held, "ctx", 1)
    anchor_k = jnp.where(even, held, got)
    anchor_v = jnp.where(even, got, held)

    partials = host_partials(spot, own_len, pieces, ctx_keys, ctx_values, heads)
    parts = [partials[0]] + [swap(partials[k], "ctx", k << 1) for k in range(1, SPREAD)]
    one = merged(parts, HD)
    for b in other_bits[1:]:
        one = merged([one, swap(one, "ctx", 1 << b)], HD)
    chunk = finished([one, swap(one, "ctx", 1)], HD, tokens)
    chunks = [chunk] + [swap(chunk, "ctx", k << 1) for k in range(1, SPREAD)]
    sums = projected(spot, head, chunks, out_weight, groups)
    answer = sums[0]
    for k in range(1, groups):
        answer = answer + swap(sums[k], "head", k)
    answer = answer.astype(BF16)

    tile = 256
    anchor_tiles = jnp.where(is_anchor, 0, (anchor_len + tile - 1) // tile)
    lens = jnp.stack([own_len, anchor_len, anchor_tiles]).astype(jnp.int32)
    context_out = context_attention(
        lens, ctx_queries, ctx_keys, ctx_values, anchor_k, anchor_v, tk=tile
    )
    return (context_out, answer)


def solution(mesh):
    placed = (
        P("ctx", "head"),
        P("ctx", "head"),
        P("ctx", "head"),
        P("ctx", "head"),
        P("head", "ctx"),
        P(),
        P(),
    )
    return jax.shard_map(
        per_device,
        mesh=mesh,
        in_specs=placed,
        out_specs=(P("ctx", "head"), P("head", "ctx")),
        check_vma=False,
    )
```

```python
import functools

import jax
import jax.numpy as jnp
from jax import lax
from jax.experimental import pallas as pl
from jax.experimental.pallas import tpu as pltpu
from jax.sharding import PartitionSpec as P

HD = 128
CLIP_FACTOR = 2.0
NEG = -1e30
LOG2E = 1.4426950408889634
NT = (((1,), (1,)), ((), ()))
SPREAD = 4
SPREAD_BITS = (1, 2)
TAIL = 8
PIECES = 4
F32 = jnp.float32
BF16 = jnp.bfloat16


def sign_table(size):
    a = lax.broadcasted_iota(jnp.int32, (size, size), 0)
    b = lax.broadcasted_iota(jnp.int32, (size, size), 1)
    x = jnp.bitwise_and(a, b)
    parity = jnp.zeros((size, size), jnp.int32)
    for bit in range(int(size).bit_length()):
        parity = jnp.bitwise_xor(parity, jnp.bitwise_and(jnp.right_shift(x, bit), 1))
    return (1 - 2 * parity).astype(F32)


def context_kernel(blocks, lens, q_ref, k_ref, v_ref, *refs, tq, tk, hp, st):
    pieces, o_ref, ak_ref, av_ref = refs[:PIECES], refs[-3], refs[-2], refs[-1]
    me = lax.axis_index("ctx")
    own_block = blocks[me]
    own_len = lens[own_block]
    anchor_len = jnp.where(own_block == 0, 0, lens[0])
    rows, hd = k_ref.shape
    piece = rows // PIECES

    @pl.when(pl.program_id(0) == 0)
    def _():
        for k in range(PIECES):
            at = pl.multiple_of(jnp.bitwise_xor(me % PIECES, k) * piece, piece)
            ak_ref[pl.ds(at, piece), :] = pieces[k][:piece]
            av_ref[pl.ds(at, piece), :] = pieces[k][piece:]

    c = hd**-0.5 * LOG2E

    def scores(na, h, i):
        q = [q_ref[i * tq : (i + 1) * tq, (h + e) * hd : (h + e + 1) * hd] for e in range(st)]
        q = jnp.concatenate(q, axis=0)
        parts = []
        if na:
            edge = (na - 1) * tk
            sa = lax.dot_general(q, ak_ref[: na * tk], NT, preferred_element_type=F32)
            col = lax.broadcasted_iota(jnp.int32, (1, tk), 1)
            if na > 1:
                parts.append((sa[:, :edge], av_ref, 0))
            parts.append((jnp.where(col < anchor_len - edge, sa[:, edge:], NEG), av_ref, edge))
        so = lax.dot_general(q, k_ref[: (i + 1) * tq], NT, preferred_element_type=F32)
        r0 = lax.broadcasted_iota(jnp.int32, (tq, tq), 0)
        c0 = lax.broadcasted_iota(jnp.int32, (tq, tq), 1)
        seen = c0 <= r0
        d = [jnp.where(seen, so[e * tq : (e + 1) * tq, i * tq :], NEG) for e in range(st)]
        if i:
            parts.append((so[:, : i * tq], v_ref, 0))
        parts.append((jnp.concatenate(d, axis=0), v_ref, i * tq))
        return parts

    def fold(op, xs):
        return functools.reduce(
            op, [x[:, a : a + 128] for x in xs for a in range(0, x.shape[1], 128)]
        )

    def finish(parts, h, i):
        m = jnp.max(fold(jnp.maximum, [p for p, _, _ in parts]), axis=1, keepdims=True)
        acc = 0.0
        powers = []
        for p, src, at in parts:
            e = jnp.exp2((p - m) * c)
            powers.append(e)
            acc = acc + jnp.dot(
                e.astype(BF16), src[at : at + p.shape[1]], preferred_element_type=F32
            )
        total = jnp.sum(fold(jnp.add, powers), axis=1, keepdims=True)
        row = lax.broadcasted_iota(jnp.int32, (tq, 1), 0) + i * tq
        for e in range(st):
            part = slice(e * tq, (e + 1) * tq)
            out = jnp.where(row < own_len, acc[part] / total[part], 0.0)
            o_ref[i * tq : (i + 1) * tq, (h + e) * hd : (h + e + 1) * hd] = out.astype(BF16)

    def body(na):
        pending = None
        for h in range(0, hp, st):
            for i in range(rows // tq):
                s = scores(na, h, i)
                if pending is not None:
                    finish(*pending)
                pending = (s, h, i)
        finish(*pending)

    top = rows // tk
    for na in range(1, top + 1):
        above = anchor_len > (na - 1) * tk if na > 1 else True
        below = anchor_len <= na * tk if na < top else True
        pl.when(jnp.logical_and(above, below))(functools.partial(body, na))


def context_attention(blocks, lens, q, k, v, anchors, first, count, into, tq=128, tk=512, hp=2, st=2):
    rows, width = q.shape
    hd = k.shape[1]
    heads = width // hd
    full = pl.BlockSpec((rows, hd), lambda h, *_: (0, 0))
    piece = pl.BlockSpec((2 * rows // PIECES, hd), lambda h, *_: (0, 0))
    wide = pl.BlockSpec((rows, hp * hd), lambda h, *_: (0, h + first // hp))
    more = [] if into is None else [into]
    return pl.pallas_call(
        functools.partial(context_kernel, tq=tq, tk=tk, hp=hp, st=st),
        grid_spec=pltpu.PrefetchScalarGridSpec(
            num_scalar_prefetch=2,
            grid=(count // hp,),
            in_specs=[wide, full, full] + [piece] * PIECES + [pl.BlockSpec(memory_space=pl.ANY)] * len(more),
            out_specs=wide,
            scratch_shapes=[pltpu.VMEM((rows, hd), BF16)] * 2,
        ),
        input_output_aliases={5 + PIECES: 0} if more else {},
        out_shape=jax.ShapeDtypeStruct(q.shape, q.dtype),
        compiler_params=pltpu.CompilerParams(vmem_limit_bytes=40 << 20),
        cost_estimate=pl.CostEstimate(
            flops=6 * count * rows * rows * hd,
            bytes_accessed=4 * rows * count * hd + 8 * rows * hd,
            transcendentals=count * rows * rows * 3 // 2,
        ),
        name="context_attention",
    )(blocks, lens, q, k, v, *anchors, *more)


def deal_kernel(k_ref, v_ref, *outs):
    mine = lax.axis_index("ctx") % PIECES
    piece = k_ref.shape[0] // PIECES
    for k in range(PIECES):
        at = pl.multiple_of(jnp.bitwise_xor(mine, k) * piece, piece)
        outs[k][:piece, :] = k_ref[pl.ds(at, piece), :]
        outs[k][piece:, :] = v_ref[pl.ds(at, piece), :]


def dealt(keys, values):
    whole = pl.BlockSpec(memory_space=pltpu.VMEM)
    shape = jax.ShapeDtypeStruct((2 * keys.shape[0] // PIECES, keys.shape[1]), keys.dtype)
    return pl.pallas_call(
        deal_kernel,
        in_specs=[whole] * 2,
        out_specs=[whole] * PIECES,
        out_shape=[shape] * PIECES,
        name="deal_pieces",
    )(keys, values)


def partial_kernel(host_block, lens, *refs, hd, step, blocks):
    q_refs, (k_ref, v_ref), outs, (q_all,) = (
        refs[:SPREAD],
        refs[SPREAD : SPREAD + 2],
        refs[SPREAD + 2 : -1],
        refs[-1:],
    )
    me = lax.axis_index("ctx")
    spot = jnp.bitwise_and(jnp.right_shift(me, 1), SPREAD - 1)
    own_len = lens[host_block[me]]
    tokens, width = q_all.shape
    per = width // hd // SPREAD
    scale = hd**-0.5
    table = sign_table(hd)
    table16 = table.astype(BF16)
    for k in range(SPREAD):
        for x in range(blocks):
            at = pl.multiple_of((x * SPREAD + jnp.bitwise_xor(spot, k)) * step, step)
            q_all[pl.ds(at, step), :] = q_refs[k][x * step : (x + 1) * step, :]

    def store(ref):
        r = jnp.dot(ref[...], table16, preferred_element_type=F32) * scale
        ceiling = CLIP_FACTOR * jnp.sqrt(jnp.mean(r * r, axis=-1, keepdims=True))
        return jnp.clip(r, -ceiling, ceiling)

    key_store = store(k_ref).astype(BF16)
    value_turned = store(v_ref).T.astype(BF16)
    rows = k_ref.shape[0]
    usable = lax.broadcasted_iota(jnp.int32, (rows, 1), 0) < own_len
    for k in range(SPREAD):
        at = pl.multiple_of(jnp.bitwise_xor(spot, k) * (per * hd), per * hd)
        q = q_all[:, pl.ds(at, per * hd)]
        q = jnp.concatenate([q[:, e * hd : (e + 1) * hd] for e in range(per)], axis=0)
        rot = (jnp.dot(q, table16, preferred_element_type=F32) * scale).astype(BF16)
        s = lax.dot_general(key_store, rot, NT, preferred_element_type=F32) * scale
        s = jnp.where(usable, s, NEG)
        m = jnp.max(s, axis=0, keepdims=True)
        p = jnp.exp(s - m)
        total = jnp.sum(p, axis=0, keepdims=True)
        outs[k][:hd, :] = jnp.dot(value_turned, p.astype(BF16), preferred_element_type=F32)
        outs[k][hd : hd + 1, :] = m
        outs[k][hd + 1 : hd + 2, :] = total
        outs[k][hd + 2 :, :] = jnp.zeros((TAIL - 2, q.shape[0]), F32)


def host_partials(host_block, lens, pieces, keys, values, heads):
    hd = keys.shape[1]
    width = pieces[0].shape[1]
    tokens = SPREAD * pieces[0].shape[0]
    blocks = pieces[0].shape[0] // 16
    shape = jax.ShapeDtypeStruct((hd + TAIL, tokens * heads // SPREAD), F32)
    whole = pl.BlockSpec(memory_space=pltpu.VMEM)
    return pl.pallas_call(
        functools.partial(partial_kernel, hd=hd, step=16, blocks=blocks),
        in_specs=[pl.BlockSpec(memory_space=pltpu.SMEM)] * 2 + [whole] * (SPREAD + 2),
        out_specs=[whole] * SPREAD,
        out_shape=[shape] * SPREAD,
        scratch_shapes=[pltpu.VMEM((tokens, width), BF16)],
        compiler_params=pltpu.CompilerParams(vmem_limit_bytes=24 << 20),
        name="host_partials",
    )(host_block, lens, *pieces, keys, values)


def merge_values(parts, hd):
    maxima = [p[hd : hd + 1, :] for p in parts]
    overall = functools.reduce(jnp.maximum, maxima)
    factors = [jnp.exp(m - overall) for m in maxima]
    out = sum(p[:hd, :] * f for p, f in zip(parts, factors))
    total = sum(p[hd + 1 : hd + 2, :] * f for p, f in zip(parts, factors))
    return overall, total, out


def merge_kernel(*refs, hd):
    o_ref = refs[-1]
    overall, total, out = merge_values(refs[:-1], hd)
    o_ref[:hd, :] = out
    o_ref[hd : hd + 1, :] = overall
    o_ref[hd + 1 : hd + 2, :] = total
    o_ref[hd + 2 :, :] = jnp.zeros((TAIL - 2, out.shape[1]), F32)


def merged(parts, hd):
    whole = pl.BlockSpec(memory_space=pltpu.VMEM)
    return pl.pallas_call(
        functools.partial(merge_kernel, hd=hd),
        in_specs=[whole] * len(parts),
        out_specs=whole,
        out_shape=jax.ShapeDtypeStruct(parts[0].shape, F32),
        name="merge_partials",
    )(*parts)


def finish_kernel(*refs, hd, tokens):
    o_ref = refs[-1]
    _, total, out = merge_values(refs[:-1], hd)
    turned = jnp.dot(
        sign_table(hd),
        out / total,
        preferred_element_type=F32,
        precision=lax.Precision.HIGHEST,
    )
    turned = (turned * hd**-0.5).T
    for e in range(turned.shape[0] // tokens):
        o_ref[:, e * hd : (e + 1) * hd] = turned[e * tokens : (e + 1) * tokens].astype(BF16)


def finished(parts, hd, tokens):
    whole = pl.BlockSpec(memory_space=pltpu.VMEM)
    per = parts[0].shape[1] // tokens
    return pl.pallas_call(
        functools.partial(finish_kernel, hd=hd, tokens=tokens),
        in_specs=[whole] * len(parts),
        out_specs=whole,
        out_shape=jax.ShapeDtypeStruct((tokens, per * hd), BF16),
        name="finish_queries",
    )(*parts)


def project_kernel(*refs, groups):
    a_refs, w_ref, outs, total = refs[:SPREAD], refs[SPREAD], refs[SPREAD + 1 : -1], refs[-1]
    spot = jnp.bitwise_and(jnp.right_shift(lax.axis_index("ctx"), 1), SPREAD - 1)
    head = lax.axis_index("head")
    depth = a_refs[0].shape[1]
    acc = 0.0
    for k in range(SPREAD):
        at = pl.multiple_of(jnp.bitwise_xor(spot, k) * depth, depth)
        acc = acc + jnp.dot(a_refs[k][...], w_ref[pl.ds(at, depth), :], preferred_element_type=F32)
    total[...] = acc
    rows = total.shape[0] // groups
    for k in range(groups):
        at = pl.multiple_of(jnp.bitwise_xor(head, k) * rows, rows)
        outs[k][...] = total[pl.ds(at, rows), :]


def projected(chunks, weight, groups):
    tokens = chunks[0].shape[0]
    columns = weight.shape[1]
    whole = pl.BlockSpec(memory_space=pltpu.VMEM)
    return pl.pallas_call(
        functools.partial(project_kernel, groups=groups),
        in_specs=[whole] * (SPREAD + 1),
        out_specs=[whole] * groups,
        out_shape=[jax.ShapeDtypeStruct((tokens // groups, columns), F32)] * groups,
        scratch_shapes=[pltpu.VMEM((tokens, columns), F32)],
        compiler_params=pltpu.CompilerParams(vmem_limit_bytes=16 << 20),
        name="project",
    )(*chunks, weight)


def swap(x, axis, flip):
    size = lax.axis_size(axis)
    return lax.ppermute(x, axis, [(i, i ^ flip) for i in range(size)])


def per_device(
    ctx_queries, ctx_keys, ctx_values, new_queries, out_weight, host_block, block_lengths
):
    hosts = lax.axis_size("ctx")
    groups = lax.axis_size("head")
    bits = hosts.bit_length() - 1
    other_bits = [b for b in range(bits) if b not in SPREAD_BITS]
    heads = ctx_queries.shape[1] // HD
    tokens = new_queries.shape[0] * hosts
    me = lax.axis_index("ctx").astype(jnp.int32)
    host_ids = jnp.arange(hosts, dtype=jnp.int32)
    root = jnp.sum(jnp.where(host_block == 0, host_ids, 0))
    differ = jnp.bitwise_xor(root, me)

    def bit(value, b):
        return jnp.bitwise_and(jnp.right_shift(value, b), 1)

    piece = new_queries
    for b in other_bits:
        got = swap(piece, "ctx", 1 << b)
        low = bit(me, b) == 0
        piece = jnp.concatenate([jnp.where(low, piece, got), jnp.where(low, got, piece)], axis=0)
    pieces = [piece] + [swap(piece, "ctx", k << 1) for k in range(1, SPREAD)]

    deal = dealt(ctx_keys, ctx_values)
    deal = [deal[0]] + [swap(deal[k], "ctx", k) for k in range(1, PIECES)]
    held = lax.select_n(jnp.bitwise_and(differ, PIECES - 1), *deal)
    pieces[0], held = lax.optimization_barrier((pieces[0], held))
    for b in range(2, bits):
        held = jnp.where(bit(differ, b) == 0, held, swap(held, "ctx", 1 << b))

    partials = host_partials(host_block, block_lengths, pieces, ctx_keys, ctx_values, heads)
    parts = [partials[0]] + [swap(partials[k], "ctx", k << 1) for k in range(1, SPREAD)]
    parts[0], held = lax.optimization_barrier((parts[0], held))
    anchors = [held] + [swap(held, "ctx", k) for k in range(1, PIECES)]
    one = merged(parts, HD)
    for b in other_bits[1:]:
        one = merged([one, swap(one, "ctx", 1 << b)], HD)
    chunk = finished([one, swap(one, "ctx", 1)], HD, tokens)
    chunks = [chunk] + [swap(chunk, "ctx", k << 1) for k in range(1, SPREAD)]

    def attend(queries, first, into):
        return context_attention(
            host_block, block_lengths, queries, ctx_keys, ctx_values, anchors, first, heads // 2, into
        )

    queries, _ = lax.optimization_barrier((ctx_queries, chunk))
    context_out = attend(queries, 0, None)
    chunks[0], context_out = lax.optimization_barrier((chunks[0], context_out))
    sums = projected(chunks, out_weight, groups)
    queries, _ = lax.optimization_barrier((queries, sums[0]))
    context_out = attend(queries, heads // 2, context_out)
    answer = sums[0]
    for k in range(1, groups):
        answer = answer + swap(sums[k], "head", k)
    answer = answer.astype(BF16)
    return (context_out, answer)


def solution(mesh):
    placed = (
        P("ctx", "head"),
        P("ctx", "head"),
        P("ctx", "head"),
        P("ctx", "head"),
        P("head", "ctx"),
        P(),
        P(),
    )
    return jax.shard_map(
        per_device,
        mesh=mesh,
        in_specs=placed,
        out_specs=(P("ctx", "head"), P("head", "ctx")),
        check_vma=False,
    )
```

```python
import functools

import jax
import jax.numpy as jnp
from jax import lax
from jax.experimental import pallas as pl
from jax.experimental.pallas import tpu as pltpu
from jax.sharding import PartitionSpec as P

HD = 128
CLIP_FACTOR = 2.0
NEG = -1e30
LOG2E = 1.4426950408889634
NT = (((1,), (1,)), ((), ()))
SPREAD = 4
SPREAD_BITS = (1, 2)
TAIL = 8
PIECES = 4
F32 = jnp.float32
BF16 = jnp.bfloat16


def sign_table(size):
    a = lax.broadcasted_iota(jnp.int32, (size, size), 0)
    b = lax.broadcasted_iota(jnp.int32, (size, size), 1)
    x = jnp.bitwise_and(a, b)
    parity = jnp.zeros((size, size), jnp.int32)
    for bit in range(int(size).bit_length()):
        parity = jnp.bitwise_xor(parity, jnp.bitwise_and(jnp.right_shift(x, bit), 1))
    return (1 - 2 * parity).astype(F32)


def context_kernel(blocks, lens, q_ref, k_ref, v_ref, *refs, tq, tk, hp, st):
    pieces, o_ref, ak_ref, av_ref = refs[:PIECES], refs[-3], refs[-2], refs[-1]
    me = lax.axis_index("ctx")
    own_block = blocks[me]
    own_len = lens[own_block]
    anchor_len = jnp.where(own_block == 0, 0, lens[0])
    rows, hd = k_ref.shape
    piece = rows // PIECES

    @pl.when(pl.program_id(0) == 0)
    def _():
        for k in range(PIECES):
            at = pl.multiple_of(jnp.bitwise_xor(me % PIECES, k) * piece, piece)
            ak_ref[pl.ds(at, piece), :] = pieces[k][:piece]
            av_ref[pl.ds(at, piece), :] = pieces[k][piece:]

    c = hd**-0.5 * LOG2E

    def scores(na, h, i):
        q = [q_ref[i * tq : (i + 1) * tq, (h + e) * hd : (h + e + 1) * hd] for e in range(st)]
        q = jnp.concatenate(q, axis=0)
        parts = []
        if na:
            edge = (na - 1) * tk
            sa = lax.dot_general(q, ak_ref[: na * tk], NT, preferred_element_type=F32)
            col = lax.broadcasted_iota(jnp.int32, (1, tk), 1)
            if na > 1:
                parts.append((sa[:, :edge], av_ref, 0))
            parts.append((jnp.where(col < anchor_len - edge, sa[:, edge:], NEG), av_ref, edge))
        so = lax.dot_general(q, k_ref[: (i + 1) * tq], NT, preferred_element_type=F32)
        r0 = lax.broadcasted_iota(jnp.int32, (tq, tq), 0)
        c0 = lax.broadcasted_iota(jnp.int32, (tq, tq), 1)
        seen = c0 <= r0
        d = [jnp.where(seen, so[e * tq : (e + 1) * tq, i * tq :], NEG) for e in range(st)]
        if i:
            parts.append((so[:, : i * tq], v_ref, 0))
        parts.append((jnp.concatenate(d, axis=0), v_ref, i * tq))
        return parts

    def fold(op, xs):
        return functools.reduce(
            op, [x[:, a : a + 128] for x in xs for a in range(0, x.shape[1], 128)]
        )

    def finish(parts, h, i):
        m = jnp.max(fold(jnp.maximum, [p for p, _, _ in parts]), axis=1, keepdims=True)
        acc = 0.0
        powers = []
        for p, src, at in parts:
            e = jnp.exp2((p - m) * c)
            powers.append(e)
            acc = acc + jnp.dot(
                e.astype(BF16), src[at : at + p.shape[1]], preferred_element_type=F32
            )
        total = jnp.sum(fold(jnp.add, powers), axis=1, keepdims=True)
        row = lax.broadcasted_iota(jnp.int32, (tq, 1), 0) + i * tq
        for e in range(st):
            part = slice(e * tq, (e + 1) * tq)
            out = jnp.where(row < own_len, acc[part] / total[part], 0.0)
            o_ref[i * tq : (i + 1) * tq, (h + e) * hd : (h + e + 1) * hd] = out.astype(BF16)

    def body(na):
        pending = None
        for h in range(0, hp, st):
            for i in range(rows // tq):
                s = scores(na, h, i)
                if pending is not None:
                    finish(*pending)
                pending = (s, h, i)
        finish(*pending)

    top = rows // tk
    for na in range(1, top + 1):
        above = anchor_len > (na - 1) * tk if na > 1 else True
        below = anchor_len <= na * tk if na < top else True
        pl.when(jnp.logical_and(above, below))(functools.partial(body, na))


def context_attention(blocks, lens, q, k, v, anchors, first, count, into, tq=128, tk=512, hp=2, st=2):
    rows, width = q.shape
    hd = k.shape[1]
    heads = width // hd
    full = pl.BlockSpec((rows, hd), lambda h, *_: (0, 0))
    piece = pl.BlockSpec((2 * rows // PIECES, hd), lambda h, *_: (0, 0))
    wide = pl.BlockSpec((rows, hp * hd), lambda h, *_: (0, h + first // hp))
    more = [] if into is None else [into]
    return pl.pallas_call(
        functools.partial(context_kernel, tq=tq, tk=tk, hp=hp, st=st),
        grid_spec=pltpu.PrefetchScalarGridSpec(
            num_scalar_prefetch=2,
            grid=(count // hp,),
            in_specs=[wide, full, full] + [piece] * PIECES + [pl.BlockSpec(memory_space=pl.ANY)] * len(more),
            out_specs=wide,
            scratch_shapes=[pltpu.VMEM((rows, hd), BF16)] * 2,
        ),
        input_output_aliases={5 + PIECES: 0} if more else {},
        out_shape=jax.ShapeDtypeStruct(q.shape, q.dtype),
        compiler_params=pltpu.CompilerParams(vmem_limit_bytes=24 << 20),
        cost_estimate=pl.CostEstimate(
            flops=6 * count * rows * rows * hd,
            bytes_accessed=4 * rows * count * hd + 8 * rows * hd,
            transcendentals=count * rows * rows * 3 // 2,
        ),
        name="context_attention",
    )(blocks, lens, q, k, v, *anchors, *more)


def deal_kernel(k_ref, v_ref, q_ref, *outs):
    mine = lax.axis_index("ctx") % PIECES
    piece = k_ref.shape[0] // PIECES
    hd = k_ref.shape[1]
    q = q_ref[...].astype(F32)
    q = [q[:, a : a + hd] for a in range(0, q.shape[1], hd)]
    q = jnp.concatenate(q, axis=0).astype(BF16)
    for k in range(PIECES):
        at = pl.multiple_of(jnp.bitwise_xor(mine, k) * piece, piece)
        outs[k][:piece, :] = k_ref[pl.ds(at, piece), :]
        outs[k][piece : 2 * piece, :] = v_ref[pl.ds(at, piece), :]
        outs[k][2 * piece :, :] = q


def dealt(keys, values, queries):
    hd = keys.shape[1]
    whole = pl.BlockSpec(memory_space=pltpu.VMEM)
    rows = 2 * keys.shape[0] // PIECES + queries.size // hd
    return pl.pallas_call(
        deal_kernel,
        in_specs=[whole] * 3,
        out_specs=[whole] * PIECES,
        out_shape=[jax.ShapeDtypeStruct((rows, hd), keys.dtype)] * PIECES,
        compiler_params=pltpu.CompilerParams(vmem_limit_bytes=6 << 20),
        name="deal_pieces",
    )(keys, values, queries)


def differing(host_block):
    root = 0
    for i in range(host_block.shape[0]):
        root = root + jnp.where(host_block[i] == 0, i, 0)
    return jnp.bitwise_xor(root, lax.axis_index("ctx"))


def regroup_kernel(host_block, *refs, body):
    parts, o_ref = refs[:-1], refs[-1]
    differ = jnp.bitwise_and(differing(host_block), PIECES - 1)
    mine = lax.axis_index("ctx") % PIECES
    count = parts[0].shape[0] - body
    for k in range(PIECES):

        @pl.when(differ == k)
        def _():
            o_ref[:body, :] = parts[k][:body, :]

        at = pl.multiple_of(body + jnp.bitwise_xor(mine, k) * count, 16)
        o_ref[pl.ds(at, count), :] = parts[k][body:, :]


def regrouped(host_block, parts, body):
    whole = pl.BlockSpec(memory_space=pltpu.VMEM)
    rows, hd = parts[0].shape
    return pl.pallas_call(
        functools.partial(regroup_kernel, body=body),
        in_specs=[pl.BlockSpec(memory_space=pltpu.SMEM)] + [whole] * PIECES,
        out_specs=whole,
        out_shape=jax.ShapeDtypeStruct((body + PIECES * (rows - body), hd), parts[0].dtype),
        compiler_params=pltpu.CompilerParams(vmem_limit_bytes=4 << 20),
        name="regroup",
    )(host_block, *parts)


def far_kernel(host_block, own, got, *outs, body, bit, last):
    mine = jnp.bitwise_and(jnp.right_shift(lax.axis_index("ctx"), bit), 1)
    differ = jnp.bitwise_and(jnp.right_shift(differing(host_block), bit), 1)
    held, queries = outs if last else (outs[0].at[:body, :], outs[0].at[body:, :])
    count = own.shape[0] - body

    @pl.when(differ == 0)
    def _():
        held[...] = own[:body, :]

    @pl.when(differ == 1)
    def _():
        held[...] = got[:body, :]

    queries[pl.ds(pl.multiple_of(mine * count, 16), count), :] = own[body:, :]
    queries[pl.ds(pl.multiple_of((1 - mine) * count, 16), count), :] = got[body:, :]


def far_merged(host_block, own, got, body, bit, last):
    whole = pl.BlockSpec(memory_space=pltpu.VMEM)
    rows, hd = own.shape
    sizes = [body, 2 * (rows - body)]
    sizes = sizes if last else [sum(sizes)]
    return pl.pallas_call(
        functools.partial(far_kernel, body=body, bit=bit, last=last),
        in_specs=[pl.BlockSpec(memory_space=pltpu.SMEM)] + [whole] * 2,
        out_specs=[whole] * len(sizes),
        out_shape=[jax.ShapeDtypeStruct((r, hd), own.dtype) for r in sizes],
        compiler_params=pltpu.CompilerParams(vmem_limit_bytes=4 << 20),
        name="far_merge",
    )(host_block, own, got)


def store_kernel(k_ref, v_ref, key_ref, value_ref):
    hd = k_ref.shape[1]
    table = sign_table(hd).astype(BF16)

    def store(ref):
        r = jnp.dot(ref[...], table, preferred_element_type=F32) * hd**-0.5
        ceiling = CLIP_FACTOR * jnp.sqrt(jnp.mean(r * r, axis=-1, keepdims=True))
        return jnp.clip(r, -ceiling, ceiling)

    key_ref[...] = store(k_ref).astype(BF16)
    value_ref[...] = store(v_ref).T.astype(BF16)


def stored(keys, values):
    whole = pl.BlockSpec(memory_space=pltpu.VMEM)
    return pl.pallas_call(
        store_kernel,
        in_specs=[whole] * 2,
        out_specs=[whole] * 2,
        out_shape=[
            jax.ShapeDtypeStruct(keys.shape, BF16),
            jax.ShapeDtypeStruct(values.shape[::-1], BF16),
        ],
        compiler_params=pltpu.CompilerParams(vmem_limit_bytes=8 << 20),
        name="rotate_store",
    )(keys, values)


def partial_kernel(host_block, lens, q_ref, key_ref, value_ref, *refs, per, step):
    outs, turned = refs[:-1], refs[-1]
    me = lax.axis_index("ctx")
    spot = jnp.bitwise_and(jnp.right_shift(me, 1), SPREAD - 1)
    own_len = lens[host_block[me]]
    rows, hd = key_ref.shape
    scale = hd**-0.5
    hosts = host_block.shape[0]
    turned[...] = (
        jnp.dot(q_ref[...], sign_table(hd).astype(BF16), preferred_element_type=F32) * scale
    )
    usable = lax.broadcasted_iota(jnp.int32, (rows, 1), 0) < own_len
    for k in range(SPREAD):
        first = jnp.bitwise_xor(spot, k) * (per * step)
        rot = []
        for e in range(per):
            for c in range(hosts):
                at = pl.multiple_of(first + (c * SPREAD * per + e) * step, step)
                rot.append(turned[pl.ds(at, step), :])
        rot = jnp.concatenate(rot, axis=0).astype(BF16)
        s = lax.dot_general(key_ref[...], rot, NT, preferred_element_type=F32) * scale
        s = jnp.where(usable, s, NEG)
        m = jnp.max(s, axis=0, keepdims=True)
        p = jnp.exp(s - m)
        total = jnp.sum(p, axis=0, keepdims=True)
        outs[k][:hd, :] = jnp.dot(value_ref[...], p.astype(BF16), preferred_element_type=F32)
        outs[k][hd : hd + 1, :] = m
        outs[k][hd + 1 : hd + 2, :] = total
        outs[k][hd + 2 :, :] = jnp.zeros((TAIL - 2, rot.shape[0]), F32)


def host_partials(host_block, lens, queries, key_store, value_store, heads, step):
    hd = key_store.shape[1]
    rows = queries.shape[0]
    shape = jax.ShapeDtypeStruct((hd + TAIL, rows // SPREAD), F32)
    whole = pl.BlockSpec(memory_space=pltpu.VMEM)
    return pl.pallas_call(
        functools.partial(partial_kernel, per=heads // SPREAD, step=step),
        in_specs=[pl.BlockSpec(memory_space=pltpu.SMEM)] * 2 + [whole] * 3,
        out_specs=[whole] * SPREAD,
        out_shape=[shape] * SPREAD,
        scratch_shapes=[pltpu.VMEM((rows, hd), F32)],
        compiler_params=pltpu.CompilerParams(vmem_limit_bytes=16 << 20),
        name="host_partials",
    )(host_block, lens, queries, key_store, value_store)


def merge_values(parts, hd):
    maxima = [p[hd : hd + 1, :] for p in parts]
    overall = functools.reduce(jnp.maximum, maxima)
    factors = [jnp.exp(m - overall) for m in maxima]
    out = sum(p[:hd, :] * f for p, f in zip(parts, factors))
    total = sum(p[hd + 1 : hd + 2, :] * f for p, f in zip(parts, factors))
    return overall, total, out


def merge_kernel(*refs, hd):
    o_ref = refs[-1]
    overall, total, out = merge_values(refs[:-1], hd)
    o_ref[:hd, :] = out
    o_ref[hd : hd + 1, :] = overall
    o_ref[hd + 1 : hd + 2, :] = total
    o_ref[hd + 2 :, :] = jnp.zeros((TAIL - 2, out.shape[1]), F32)


def merged(parts, hd):
    whole = pl.BlockSpec(memory_space=pltpu.VMEM)
    return pl.pallas_call(
        functools.partial(merge_kernel, hd=hd),
        in_specs=[whole] * len(parts),
        out_specs=whole,
        out_shape=jax.ShapeDtypeStruct(parts[0].shape, F32),
        compiler_params=pltpu.CompilerParams(vmem_limit_bytes=4 << 20),
        name="merge_partials",
    )(*parts)


def finish_kernel(*refs, hd, tokens):
    o_ref = refs[-1]
    _, total, out = merge_values(refs[:-1], hd)
    turned = jnp.dot(
        sign_table(hd),
        out / total,
        preferred_element_type=F32,
        precision=lax.Precision.HIGHEST,
    )
    turned = (turned * hd**-0.5).T
    for e in range(turned.shape[0] // tokens):
        o_ref[:, e * hd : (e + 1) * hd] = turned[e * tokens : (e + 1) * tokens].astype(BF16)


def finished(parts, hd, tokens):
    whole = pl.BlockSpec(memory_space=pltpu.VMEM)
    per = parts[0].shape[1] // tokens
    return pl.pallas_call(
        functools.partial(finish_kernel, hd=hd, tokens=tokens),
        in_specs=[whole] * len(parts),
        out_specs=whole,
        out_shape=jax.ShapeDtypeStruct((tokens, per * hd), BF16),
        compiler_params=pltpu.CompilerParams(vmem_limit_bytes=4 << 20),
        name="finish_queries",
    )(*parts)


def project_kernel(*refs, groups):
    a_refs, w_ref, outs, total = refs[:SPREAD], refs[SPREAD], refs[SPREAD + 1 : -1], refs[-1]
    spot = jnp.bitwise_and(jnp.right_shift(lax.axis_index("ctx"), 1), SPREAD - 1)
    head = lax.axis_index("head")
    depth = a_refs[0].shape[1]
    acc = 0.0
    for k in range(SPREAD):
        at = pl.multiple_of(jnp.bitwise_xor(spot, k) * depth, depth)
        acc = acc + jnp.dot(a_refs[k][...], w_ref[pl.ds(at, depth), :], preferred_element_type=F32)
    total[...] = acc
    rows = total.shape[0] // groups
    for k in range(groups):
        at = pl.multiple_of(jnp.bitwise_xor(head, k) * rows, rows)
        outs[k][...] = total[pl.ds(at, rows), :]


def projected(chunks, weight, groups):
    tokens = chunks[0].shape[0]
    columns = weight.shape[1]
    whole = pl.BlockSpec(memory_space=pltpu.VMEM)
    return pl.pallas_call(
        functools.partial(project_kernel, groups=groups),
        in_specs=[whole] * (SPREAD + 1),
        out_specs=[whole] * groups,
        out_shape=[jax.ShapeDtypeStruct((tokens // groups, columns), F32)] * groups,
        scratch_shapes=[pltpu.VMEM((tokens, columns), F32)],
        compiler_params=pltpu.CompilerParams(vmem_limit_bytes=8 << 20),
        name="project",
    )(*chunks, weight)


def swap(x, axis, flip):
    size = lax.axis_size(axis)
    return lax.ppermute(x, axis, [(i, i ^ flip) for i in range(size)])


def per_device(
    ctx_queries, ctx_keys, ctx_values, new_queries, out_weight, host_block, block_lengths
):
    hosts = lax.axis_size("ctx")
    groups = lax.axis_size("head")
    bits = hosts.bit_length() - 1
    other_bits = [b for b in range(bits) if b not in SPREAD_BITS]
    heads = ctx_queries.shape[1] // HD
    tokens = new_queries.shape[0] * hosts
    body = 2 * ctx_keys.shape[0] // PIECES

    deal = list(dealt(ctx_keys, ctx_values, new_queries))
    keys, values, deal[0] = lax.optimization_barrier((ctx_keys, ctx_values, deal[0]))
    key_store, value_store = stored(keys, values)
    deal = [deal[0]] + [swap(deal[k], "ctx", k) for k in range(1, PIECES)]
    deal[0], key_store = lax.optimization_barrier((deal[0], key_store))
    message = regrouped(host_block, deal, body)
    for b in range(2, bits):
        message = far_merged(host_block, message, swap(message, "ctx", 1 << b), body, b, b == bits - 1)
        message = message if b == bits - 1 else message[0]
    held, all_queries = message
    anchors = [held] + [swap(held, "ctx", k) for k in range(1, PIECES)]

    partials = host_partials(
        host_block, block_lengths, all_queries, key_store, value_store, heads, new_queries.shape[0]
    )
    parts = [partials[0]] + [swap(partials[k], "ctx", k << 1) for k in range(1, SPREAD)]
    one = merged(parts, HD)
    for b in other_bits[1:]:
        one = merged([one, swap(one, "ctx", 1 << b)], HD)
    other = swap(one, "ctx", 1)

    def attend(anchors, first, count, into):
        return context_attention(
            host_block, block_lengths, ctx_queries, ctx_keys, ctx_values, anchors, first, count, into
        )

    counts = (heads // 4, heads // 2, heads // 4)
    anchors[0], one = lax.optimization_barrier((anchors[0], one))
    context_out = attend(anchors, 0, counts[0], None)
    one, context_out = lax.optimization_barrier((one, context_out))
    chunk = finished([one, other], HD, tokens)
    chunks = [chunk] + [swap(chunk, "ctx", k << 1) for k in range(1, SPREAD)]
    anchors[0], _ = lax.optimization_barrier((anchors[0], chunk))
    context_out = attend(anchors, counts[0], counts[1], context_out)
    chunks[0], context_out = lax.optimization_barrier((chunks[0], context_out))
    sums = projected(chunks, out_weight, groups)
    anchors[0], _ = lax.optimization_barrier((anchors[0], sums[0]))
    context_out = attend(anchors, counts[0] + counts[1], counts[2], context_out)
    answer = sums[0]
    for k in range(1, groups):
        answer = answer + swap(sums[k], "head", k)
    answer = answer.astype(BF16)
    return (context_out, answer)


def solution(mesh):
    placed = (
        P("ctx", "head"),
        P("ctx", "head"),
        P("ctx", "head"),
        P("ctx", "head"),
        P("head", "ctx"),
        P(),
        P(),
    )
    return jax.shard_map(
        per_device,
        mesh=mesh,
        in_specs=placed,
        out_specs=(P("ctx", "head"), P("head", "ctx")),
        check_vma=False,
    )
```

```python
import functools

import jax
import jax.numpy as jnp
from jax import lax
from jax.experimental import pallas as pl
from jax.experimental.pallas import tpu as pltpu
from jax.sharding import PartitionSpec as P

HD = 128
CLIP_FACTOR = 2.0
NEG = -1e30
LOG2E = 1.4426950408889634
NT = (((1,), (1,)), ((), ()))
SPREAD = 4
SPREAD_BITS = (1, 2)
TAIL = 8
PIECES = 4
F32 = jnp.float32
BF16 = jnp.bfloat16


def sign_table(size):
    a = lax.broadcasted_iota(jnp.int32, (size, size), 0)
    b = lax.broadcasted_iota(jnp.int32, (size, size), 1)
    x = jnp.bitwise_and(a, b)
    parity = jnp.zeros((size, size), jnp.int32)
    for bit in range(int(size).bit_length()):
        parity = jnp.bitwise_xor(parity, jnp.bitwise_and(jnp.right_shift(x, bit), 1))
    return (1 - 2 * parity).astype(F32)


def context_kernel(blocks, lens, q_ref, k_ref, v_ref, *refs, tq, tk, hp, st):
    pieces, o_ref, ak_ref, av_ref = refs[:PIECES], refs[-3], refs[-2], refs[-1]
    me = lax.axis_index("ctx")
    own_block = blocks[me]
    own_len = lens[own_block]
    anchor_len = jnp.where(own_block == 0, 0, lens[0])
    rows, hd = k_ref.shape
    piece = rows // PIECES

    @pl.when(pl.program_id(0) == 0)
    def _():
        for k in range(PIECES):
            at = pl.multiple_of(jnp.bitwise_xor(me % PIECES, k) * piece, piece)
            ak_ref[pl.ds(at, piece), :] = pieces[k][:piece]
            av_ref[pl.ds(at, piece), :] = pieces[k][piece:]

    c = hd**-0.5 * LOG2E

    def scores(na, h, i):
        q = [q_ref[i * tq : (i + 1) * tq, (h + e) * hd : (h + e + 1) * hd] for e in range(st)]
        q = jnp.concatenate(q, axis=0)
        parts = []
        if na:
            edge = (na - 1) * tk
            sa = lax.dot_general(q, ak_ref[: na * tk], NT, preferred_element_type=F32)
            col = lax.broadcasted_iota(jnp.int32, (1, tk), 1)
            if na > 1:
                parts.append((sa[:, :edge], av_ref, 0))
            parts.append((jnp.where(col < anchor_len - edge, sa[:, edge:], NEG), av_ref, edge))
        so = lax.dot_general(q, k_ref[: (i + 1) * tq], NT, preferred_element_type=F32)
        r0 = lax.broadcasted_iota(jnp.int32, (tq, tq), 0)
        c0 = lax.broadcasted_iota(jnp.int32, (tq, tq), 1)
        seen = c0 <= r0
        d = [jnp.where(seen, so[e * tq : (e + 1) * tq, i * tq :], NEG) for e in range(st)]
        if i:
            parts.append((so[:, : i * tq], v_ref, 0))
        parts.append((jnp.concatenate(d, axis=0), v_ref, i * tq))
        return parts

    def fold(op, xs):
        return functools.reduce(
            op, [x[:, a : a + 128] for x in xs for a in range(0, x.shape[1], 128)]
        )

    def finish(parts, h, i):
        m = jnp.max(fold(jnp.maximum, [p for p, _, _ in parts]), axis=1, keepdims=True)
        acc = 0.0
        powers = []
        for p, src, at in parts:
            e = jnp.exp2((p - m) * c)
            powers.append(e)
            acc = acc + jnp.dot(
                e.astype(BF16), src[at : at + p.shape[1]], preferred_element_type=F32
            )
        total = jnp.sum(fold(jnp.add, powers), axis=1, keepdims=True)
        row = lax.broadcasted_iota(jnp.int32, (tq, 1), 0) + i * tq
        for e in range(st):
            part = slice(e * tq, (e + 1) * tq)
            out = jnp.where(row < own_len, acc[part] / total[part], 0.0)
            o_ref[i * tq : (i + 1) * tq, (h + e) * hd : (h + e + 1) * hd] = out.astype(BF16)

    def body(na):
        pending = None
        for h in range(0, hp, st):
            for i in range(rows // tq):
                s = scores(na, h, i)
                if pending is not None:
                    finish(*pending)
                pending = (s, h, i)
        finish(*pending)

    top = rows // tk
    for na in range(1, top + 1):
        above = anchor_len > (na - 1) * tk if na > 1 else True
        below = anchor_len <= na * tk if na < top else True
        pl.when(jnp.logical_and(above, below))(functools.partial(body, na))


def context_attention(blocks, lens, q, k, v, anchors, first, count, into, tq=128, tk=256, hp=2, st=2):
    rows, width = q.shape
    hd = k.shape[1]
    heads = width // hd
    full = pl.BlockSpec((rows, hd), lambda h, *_: (0, 0))
    piece = pl.BlockSpec((2 * rows // PIECES, hd), lambda h, *_: (0, 0))
    wide = pl.BlockSpec((rows, hp * hd), lambda h, *_: (0, h + first // hp))
    more = [] if into is None else [into]
    return pl.pallas_call(
        functools.partial(context_kernel, tq=tq, tk=tk, hp=hp, st=st),
        grid_spec=pltpu.PrefetchScalarGridSpec(
            num_scalar_prefetch=2,
            grid=(count // hp,),
            in_specs=[wide, full, full] + [piece] * PIECES + [pl.BlockSpec(memory_space=pl.ANY)] * len(more),
            out_specs=wide,
            scratch_shapes=[pltpu.VMEM((rows, hd), BF16)] * 2,
        ),
        input_output_aliases={5 + PIECES: 0} if more else {},
        out_shape=jax.ShapeDtypeStruct(q.shape, q.dtype),
        compiler_params=pltpu.CompilerParams(vmem_limit_bytes=24 << 20),
        cost_estimate=pl.CostEstimate(
            flops=6 * count * rows * rows * hd,
            bytes_accessed=4 * rows * count * hd + 8 * rows * hd,
            transcendentals=count * rows * rows * 3 // 2,
        ),
        name="context_attention",
    )(blocks, lens, q, k, v, *anchors, *more)


def deal_kernel(k_ref, v_ref, q_ref, *outs):
    mine = lax.axis_index("ctx") % PIECES
    piece = k_ref.shape[0] // PIECES
    hd = k_ref.shape[1]
    q = q_ref[...].astype(F32)
    q = [q[:, a : a + hd] for a in range(0, q.shape[1], hd)]
    q = jnp.concatenate(q, axis=0).astype(BF16)
    for k in range(PIECES):
        at = pl.multiple_of(jnp.bitwise_xor(mine, k) * piece, piece)
        outs[k][:piece, :] = k_ref[pl.ds(at, piece), :]
        outs[k][piece : 2 * piece, :] = v_ref[pl.ds(at, piece), :]
        outs[k][2 * piece :, :] = q


def dealt(keys, values, queries):
    hd = keys.shape[1]
    whole = pl.BlockSpec(memory_space=pltpu.VMEM)
    rows = 2 * keys.shape[0] // PIECES + queries.size // hd
    return pl.pallas_call(
        deal_kernel,
        in_specs=[whole] * 3,
        out_specs=[whole] * PIECES,
        out_shape=[jax.ShapeDtypeStruct((rows, hd), keys.dtype)] * PIECES,
        compiler_params=pltpu.CompilerParams(vmem_limit_bytes=6 << 20),
        name="deal_pieces",
    )(keys, values, queries)


def differing(host_block):
    root = 0
    for i in range(host_block.shape[0]):
        root = root + jnp.where(host_block[i] == 0, i, 0)
    return jnp.bitwise_xor(root, lax.axis_index("ctx"))


def regroup_kernel(host_block, *refs, body):
    parts, o_ref = refs[:-1], refs[-1]
    differ = jnp.bitwise_and(differing(host_block), PIECES - 1)
    mine = lax.axis_index("ctx") % PIECES
    count = parts[0].shape[0] - body
    for k in range(PIECES):

        @pl.when(differ == k)
        def _():
            o_ref[:body, :] = parts[k][:body, :]

        at = pl.multiple_of(body + jnp.bitwise_xor(mine, k) * count, 16)
        o_ref[pl.ds(at, count), :] = parts[k][body:, :]


def regrouped(host_block, parts, body):
    whole = pl.BlockSpec(memory_space=pltpu.VMEM)
    rows, hd = parts[0].shape
    return pl.pallas_call(
        functools.partial(regroup_kernel, body=body),
        in_specs=[pl.BlockSpec(memory_space=pltpu.SMEM)] + [whole] * PIECES,
        out_specs=whole,
        out_shape=jax.ShapeDtypeStruct((body + PIECES * (rows - body), hd), parts[0].dtype),
        compiler_params=pltpu.CompilerParams(vmem_limit_bytes=4 << 20),
        name="regroup",
    )(host_block, *parts)


def far_kernel(host_block, own, got, *outs, body, bit, last):
    mine = jnp.bitwise_and(jnp.right_shift(lax.axis_index("ctx"), bit), 1)
    differ = jnp.bitwise_and(jnp.right_shift(differing(host_block), bit), 1)
    held, queries = outs if last else (outs[0].at[:body, :], outs[0].at[body:, :])
    count = own.shape[0] - body

    @pl.when(differ == 0)
    def _():
        held[...] = own[:body, :]

    @pl.when(differ == 1)
    def _():
        held[...] = got[:body, :]

    queries[pl.ds(pl.multiple_of(mine * count, 16), count), :] = own[body:, :]
    queries[pl.ds(pl.multiple_of((1 - mine) * count, 16), count), :] = got[body:, :]


def far_merged(host_block, own, got, body, bit, last):
    whole = pl.BlockSpec(memory_space=pltpu.VMEM)
    rows, hd = own.shape
    sizes = [body, 2 * (rows - body)]
    sizes = sizes if last else [sum(sizes)]
    return pl.pallas_call(
        functools.partial(far_kernel, body=body, bit=bit, last=last),
        in_specs=[pl.BlockSpec(memory_space=pltpu.SMEM)] + [whole] * 2,
        out_specs=[whole] * len(sizes),
        out_shape=[jax.ShapeDtypeStruct((r, hd), own.dtype) for r in sizes],
        compiler_params=pltpu.CompilerParams(vmem_limit_bytes=4 << 20),
        name="far_merge",
    )(host_block, own, got)


def store_kernel(k_ref, v_ref, key_ref, value_ref):
    hd = k_ref.shape[1]
    table = sign_table(hd).astype(BF16)

    def store(ref):
        r = jnp.dot(ref[...], table, preferred_element_type=F32) * hd**-0.5
        ceiling = CLIP_FACTOR * jnp.sqrt(jnp.mean(r * r, axis=-1, keepdims=True))
        return jnp.clip(r, -ceiling, ceiling)

    key_ref[...] = store(k_ref).astype(BF16)
    value_ref[...] = store(v_ref).T.astype(BF16)


def stored(keys, values):
    whole = pl.BlockSpec(memory_space=pltpu.VMEM)
    return pl.pallas_call(
        store_kernel,
        in_specs=[whole] * 2,
        out_specs=[whole] * 2,
        out_shape=[
            jax.ShapeDtypeStruct(keys.shape, BF16),
            jax.ShapeDtypeStruct(values.shape[::-1], BF16),
        ],
        compiler_params=pltpu.CompilerParams(vmem_limit_bytes=8 << 20),
        name="rotate_store",
    )(keys, values)


def partial_kernel(host_block, lens, q_ref, key_ref, value_ref, *refs, per, step):
    outs, turned = refs[:-1], refs[-1]
    me = lax.axis_index("ctx")
    spot = jnp.bitwise_and(jnp.right_shift(me, 1), SPREAD - 1)
    own_len = lens[host_block[me]]
    rows, hd = key_ref.shape
    scale = hd**-0.5
    hosts = host_block.shape[0]
    turned[...] = (
        jnp.dot(q_ref[...], sign_table(hd).astype(BF16), preferred_element_type=F32) * scale
    )
    usable = lax.broadcasted_iota(jnp.int32, (rows, 1), 0) < own_len
    for k in range(SPREAD):
        first = jnp.bitwise_xor(spot, k) * (per * step)
        rot = []
        for e in range(per):
            for c in range(hosts):
                at = pl.multiple_of(first + (c * SPREAD * per + e) * step, step)
                rot.append(turned[pl.ds(at, step), :])
        rot = jnp.concatenate(rot, axis=0).astype(BF16)
        s = lax.dot_general(key_ref[...], rot, NT, preferred_element_type=F32) * scale
        s = jnp.where(usable, s, NEG)
        m = jnp.max(s, axis=0, keepdims=True)
        p = jnp.exp(s - m)
        total = jnp.sum(p, axis=0, keepdims=True)
        outs[k][:hd, :] = jnp.dot(value_ref[...], p.astype(BF16), preferred_element_type=F32)
        outs[k][hd : hd + 1, :] = m
        outs[k][hd + 1 : hd + 2, :] = total
        outs[k][hd + 2 :, :] = jnp.zeros((TAIL - 2, rot.shape[0]), F32)


def host_partials(host_block, lens, queries, key_store, value_store, heads, step):
    hd = key_store.shape[1]
    rows = queries.shape[0]
    shape = jax.ShapeDtypeStruct((hd + TAIL, rows // SPREAD), F32)
    whole = pl.BlockSpec(memory_space=pltpu.VMEM)
    return pl.pallas_call(
        functools.partial(partial_kernel, per=heads // SPREAD, step=step),
        in_specs=[pl.BlockSpec(memory_space=pltpu.SMEM)] * 2 + [whole] * 3,
        out_specs=[whole] * SPREAD,
        out_shape=[shape] * SPREAD,
        scratch_shapes=[pltpu.VMEM((rows, hd), F32)],
        compiler_params=pltpu.CompilerParams(vmem_limit_bytes=16 << 20),
        name="host_partials",
    )(host_block, lens, queries, key_store, value_store)


def merge_values(parts, hd):
    maxima = [p[hd : hd + 1, :] for p in parts]
    overall = functools.reduce(jnp.maximum, maxima)
    factors = [jnp.exp(m - overall) for m in maxima]
    out = sum(p[:hd, :] * f for p, f in zip(parts, factors))
    total = sum(p[hd + 1 : hd + 2, :] * f for p, f in zip(parts, factors))
    return overall, total, out


def merge_kernel(*refs, hd):
    o_ref = refs[-1]
    overall, total, out = merge_values(refs[:-1], hd)
    o_ref[:hd, :] = out
    o_ref[hd : hd + 1, :] = overall
    o_ref[hd + 1 : hd + 2, :] = total
    o_ref[hd + 2 :, :] = jnp.zeros((TAIL - 2, out.shape[1]), F32)


def merged(parts, hd):
    whole = pl.BlockSpec(memory_space=pltpu.VMEM)
    return pl.pallas_call(
        functools.partial(merge_kernel, hd=hd),
        in_specs=[whole] * len(parts),
        out_specs=whole,
        out_shape=jax.ShapeDtypeStruct(parts[0].shape, F32),
        compiler_params=pltpu.CompilerParams(vmem_limit_bytes=4 << 20),
        name="merge_partials",
    )(*parts)


def finish_kernel(*refs, hd, tokens):
    o_ref = refs[-1]
    _, total, out = merge_values(refs[:-1], hd)
    turned = jnp.dot(
        sign_table(hd),
        out / total,
        preferred_element_type=F32,
        precision=lax.Precision.HIGHEST,
    )
    turned = (turned * hd**-0.5).T
    for e in range(turned.shape[0] // tokens):
        o_ref[:, e * hd : (e + 1) * hd] = turned[e * tokens : (e + 1) * tokens].astype(BF16)


def finished(parts, hd, tokens):
    whole = pl.BlockSpec(memory_space=pltpu.VMEM)
    per = parts[0].shape[1] // tokens
    return pl.pallas_call(
        functools.partial(finish_kernel, hd=hd, tokens=tokens),
        in_specs=[whole] * len(parts),
        out_specs=whole,
        out_shape=jax.ShapeDtypeStruct((tokens, per * hd), BF16),
        compiler_params=pltpu.CompilerParams(vmem_limit_bytes=4 << 20),
        name="finish_queries",
    )(*parts)


def project_kernel(*refs, groups):
    a_refs, w_ref, outs, total = refs[:SPREAD], refs[SPREAD], refs[SPREAD + 1 : -1], refs[-1]
    spot = jnp.bitwise_and(jnp.right_shift(lax.axis_index("ctx"), 1), SPREAD - 1)
    head = lax.axis_index("head")
    depth = a_refs[0].shape[1]
    acc = 0.0
    for k in range(SPREAD):
        at = pl.multiple_of(jnp.bitwise_xor(spot, k) * depth, depth)
        acc = acc + jnp.dot(a_refs[k][...], w_ref[pl.ds(at, depth), :], preferred_element_type=F32)
    total[...] = acc
    rows = total.shape[0] // groups
    for k in range(groups):
        at = pl.multiple_of(jnp.bitwise_xor(head, k) * rows, rows)
        outs[k][...] = total[pl.ds(at, rows), :]


def projected(chunks, weight, groups):
    tokens = chunks[0].shape[0]
    columns = weight.shape[1]
    whole = pl.BlockSpec(memory_space=pltpu.VMEM)
    return pl.pallas_call(
        functools.partial(project_kernel, groups=groups),
        in_specs=[whole] * (SPREAD + 1),
        out_specs=[whole] * groups,
        out_shape=[jax.ShapeDtypeStruct((tokens // groups, columns), F32)] * groups,
        scratch_shapes=[pltpu.VMEM((tokens, columns), F32)],
        compiler_params=pltpu.CompilerParams(vmem_limit_bytes=8 << 20),
        name="project",
    )(*chunks, weight)


def swap(x, axis, flip):
    size = lax.axis_size(axis)
    return lax.ppermute(x, axis, [(i, i ^ flip) for i in range(size)])


def per_device(
    ctx_queries, ctx_keys, ctx_values, new_queries, out_weight, host_block, block_lengths
):
    hosts = lax.axis_size("ctx")
    groups = lax.axis_size("head")
    bits = hosts.bit_length() - 1
    other_bits = [b for b in range(bits) if b not in SPREAD_BITS]
    heads = ctx_queries.shape[1] // HD
    tokens = new_queries.shape[0] * hosts
    body = 2 * ctx_keys.shape[0] // PIECES

    deal = list(dealt(ctx_keys, ctx_values, new_queries))
    keys, values, deal[0] = lax.optimization_barrier((ctx_keys, ctx_values, deal[0]))
    key_store, value_store = stored(keys, values)
    deal = [deal[0]] + [swap(deal[k], "ctx", k) for k in range(1, PIECES)]
    deal[0], key_store = lax.optimization_barrier((deal[0], key_store))
    message = regrouped(host_block, deal, body)
    for b in range(2, bits):
        message = far_merged(host_block, message, swap(message, "ctx", 1 << b), body, b, b == bits - 1)
        message = message if b == bits - 1 else message[0]
    held, all_queries = message
    anchors = [held] + [swap(held, "ctx", k) for k in range(1, PIECES)]

    partials = host_partials(
        host_block, block_lengths, all_queries, key_store, value_store, heads, new_queries.shape[0]
    )
    parts = [partials[0]] + [swap(partials[k], "ctx", k << 1) for k in range(1, SPREAD)]
    one = merged(parts, HD)
    for b in other_bits[1:]:
        one = merged([one, swap(one, "ctx", 1 << b)], HD)
    other = swap(one, "ctx", 1)

    def attend(anchors, first, count, into):
        return context_attention(
            host_block, block_lengths, ctx_queries, ctx_keys, ctx_values, anchors, first, count, into
        )

    half = heads // 2
    chunk = finished([one, other], HD, tokens)
    chunks = [chunk] + [swap(chunk, "ctx", k << 1) for k in range(1, SPREAD)]
    anchors[0], _ = lax.optimization_barrier((anchors[0], chunk))
    context_out = attend(anchors, 0, half, None)
    chunks[0], context_out = lax.optimization_barrier((chunks[0], context_out))
    sums = projected(chunks, out_weight, groups)
    anchors[0], _ = lax.optimization_barrier((anchors[0], sums[0]))
    context_out = attend(anchors, half, half, context_out)
    answer = sums[0]
    for k in range(1, groups):
        answer = answer + swap(sums[k], "head", k)
    answer = answer.astype(BF16)
    return (context_out, answer)


def solution(mesh):
    placed = (
        P("ctx", "head"),
        P("ctx", "head"),
        P("ctx", "head"),
        P("ctx", "head"),
        P("head", "ctx"),
        P(),
        P(),
    )
    return jax.shard_map(
        per_device,
        mesh=mesh,
        in_specs=placed,
        out_specs=(P("ctx", "head"), P("head", "ctx")),
        check_vma=False,
    )
```

```python
import functools

import jax
import jax.numpy as jnp
from jax import lax
from jax.experimental import pallas as pl
from jax.experimental.pallas import tpu as pltpu
from jax.sharding import PartitionSpec as P

HD = 128
CLIP_FACTOR = 2.0
NEG = -1e30
LOG2E = 1.4426950408889634
NT = (((1,), (1,)), ((), ()))
SPREAD = 4
SPREAD_BITS = (1, 2)
TAIL = 8
PIECES = 4
F32 = jnp.float32
BF16 = jnp.bfloat16


def sign_table(size):
    a = lax.broadcasted_iota(jnp.int32, (size, size), 0)
    b = lax.broadcasted_iota(jnp.int32, (size, size), 1)
    x = jnp.bitwise_and(a, b)
    parity = jnp.zeros((size, size), jnp.int32)
    for bit in range(int(size).bit_length()):
        parity = jnp.bitwise_xor(parity, jnp.bitwise_and(jnp.right_shift(x, bit), 1))
    return (1 - 2 * parity).astype(F32)


def context_kernel(blocks, lens, q_ref, k_ref, v_ref, *refs, tq, tk, hp, st):
    pieces, o_ref, ak_ref, av_ref = refs[:PIECES], refs[-3], refs[-2], refs[-1]
    me = lax.axis_index("ctx")
    own_block = blocks[me]
    own_len = lens[own_block]
    anchor_len = jnp.where(own_block == 0, 0, lens[0])
    rows, hd = k_ref.shape
    piece = rows // PIECES

    @pl.when(pl.program_id(0) == 0)
    def _():
        for k in range(PIECES):
            at = pl.multiple_of(jnp.bitwise_xor(me % PIECES, k) * piece, piece)
            ak_ref[pl.ds(at, piece), :] = pieces[k][:piece]
            av_ref[pl.ds(at, piece), :] = pieces[k][piece:]

    c = hd**-0.5 * LOG2E

    def scores(na, h, i):
        q = [q_ref[i * tq : (i + 1) * tq, (h + e) * hd : (h + e + 1) * hd] for e in range(st)]
        q = jnp.concatenate(q, axis=0)
        parts = []
        if na:
            edge = (na - 1) * tk
            sa = lax.dot_general(q, ak_ref[: na * tk], NT, preferred_element_type=F32)
            col = lax.broadcasted_iota(jnp.int32, (1, tk), 1)
            if na > 1:
                parts.append((sa[:, :edge], av_ref, 0))
            parts.append((jnp.where(col < anchor_len - edge, sa[:, edge:], NEG), av_ref, edge))
        so = lax.dot_general(q, k_ref[: (i + 1) * tq], NT, preferred_element_type=F32)
        r0 = lax.broadcasted_iota(jnp.int32, (tq, tq), 0)
        c0 = lax.broadcasted_iota(jnp.int32, (tq, tq), 1)
        seen = c0 <= r0
        d = [jnp.where(seen, so[e * tq : (e + 1) * tq, i * tq :], NEG) for e in range(st)]
        if i:
            parts.append((so[:, : i * tq], v_ref, 0))
        parts.append((jnp.concatenate(d, axis=0), v_ref, i * tq))
        return parts

    def fold(op, xs):
        return functools.reduce(
            op, [x[:, a : a + 128] for x in xs for a in range(0, x.shape[1], 128)]
        )

    def finish(parts, h, i):
        m = jnp.max(fold(jnp.maximum, [p for p, _, _ in parts]), axis=1, keepdims=True)
        acc = 0.0
        powers = []
        for p, src, at in parts:
            e = jnp.exp2((p - m) * c)
            powers.append(e)
            acc = acc + jnp.dot(
                e.astype(BF16), src[at : at + p.shape[1]], preferred_element_type=F32
            )
        total = jnp.sum(fold(jnp.add, powers), axis=1, keepdims=True)
        row = lax.broadcasted_iota(jnp.int32, (tq, 1), 0) + i * tq
        for e in range(st):
            part = slice(e * tq, (e + 1) * tq)
            out = jnp.where(row < own_len, acc[part] / total[part], 0.0)
            o_ref[i * tq : (i + 1) * tq, (h + e) * hd : (h + e + 1) * hd] = out.astype(BF16)

    def body(na):
        pending = None
        for h in range(0, hp, st):
            for i in range(rows // tq):
                s = scores(na, h, i)
                if pending is not None:
                    finish(*pending)
                pending = (s, h, i)
        finish(*pending)

    top = rows // tk
    for na in range(1, top + 1):
        above = anchor_len > (na - 1) * tk if na > 1 else True
        below = anchor_len <= na * tk if na < top else True
        pl.when(jnp.logical_and(above, below))(functools.partial(body, na))


def context_attention(blocks, lens, q, k, v, anchors, first, count, into, tq=128, tk=256, hp=2, st=2):
    rows, width = q.shape
    hd = k.shape[1]
    heads = width // hd
    full = pl.BlockSpec((rows, hd), lambda h, *_: (0, 0))
    piece = pl.BlockSpec((2 * rows // PIECES, hd), lambda h, *_: (0, 0))
    wide = pl.BlockSpec((rows, hp * hd), lambda h, *_: (0, h + first // hp))
    more = [] if into is None else [into]
    return pl.pallas_call(
        functools.partial(context_kernel, tq=tq, tk=tk, hp=hp, st=st),
        grid_spec=pltpu.PrefetchScalarGridSpec(
            num_scalar_prefetch=2,
            grid=(count // hp,),
            in_specs=[wide, full, full] + [piece] * PIECES + [pl.BlockSpec(memory_space=pl.ANY)] * len(more),
            out_specs=wide,
            scratch_shapes=[pltpu.VMEM((rows, hd), BF16)] * 2,
        ),
        input_output_aliases={5 + PIECES: 0} if more else {},
        out_shape=jax.ShapeDtypeStruct(q.shape, q.dtype),
        compiler_params=pltpu.CompilerParams(vmem_limit_bytes=24 << 20),
        cost_estimate=pl.CostEstimate(
            flops=6 * count * rows * rows * hd,
            bytes_accessed=4 * rows * count * hd + 8 * rows * hd,
            transcendentals=count * rows * rows * 3 // 2,
        ),
        name="context_attention",
    )(blocks, lens, q, k, v, *anchors, *more)


def deal_kernel(k_ref, v_ref, q_ref, *outs):
    mine = lax.axis_index("ctx") % PIECES
    piece = k_ref.shape[0] // PIECES
    hd = k_ref.shape[1]
    q = q_ref[...].astype(F32)
    q = [q[:, a : a + hd] for a in range(0, q.shape[1], hd)]
    q = jnp.concatenate(q, axis=0).astype(BF16)
    for k in range(PIECES):
        at = pl.multiple_of(jnp.bitwise_xor(mine, k) * piece, piece)
        outs[k][:piece, :] = k_ref[pl.ds(at, piece), :]
        outs[k][piece : 2 * piece, :] = v_ref[pl.ds(at, piece), :]
        outs[k][2 * piece :, :] = q


def dealt(keys, values, queries):
    hd = keys.shape[1]
    whole = pl.BlockSpec(memory_space=pltpu.VMEM)
    rows = 2 * keys.shape[0] // PIECES + queries.size // hd
    return pl.pallas_call(
        deal_kernel,
        in_specs=[whole] * 3,
        out_specs=[whole] * PIECES,
        out_shape=[jax.ShapeDtypeStruct((rows, hd), keys.dtype)] * PIECES,
        compiler_params=pltpu.CompilerParams(vmem_limit_bytes=6 << 20),
        name="deal_pieces",
    )(keys, values, queries)


def differing(host_block):
    root = 0
    for i in range(host_block.shape[0]):
        root = root + jnp.where(host_block[i] == 0, i, 0)
    return jnp.bitwise_xor(root, lax.axis_index("ctx"))


def regroup_kernel(host_block, *refs, body):
    parts, o_ref = refs[:-1], refs[-1]
    differ = jnp.bitwise_and(differing(host_block), PIECES - 1)
    mine = lax.axis_index("ctx") % PIECES
    count = parts[0].shape[0] - body
    for k in range(PIECES):

        @pl.when(differ == k)
        def _():
            o_ref[:body, :] = parts[k][:body, :]

        at = pl.multiple_of(body + jnp.bitwise_xor(mine, k) * count, 16)
        o_ref[pl.ds(at, count), :] = parts[k][body:, :]


def regrouped(host_block, parts, body):
    whole = pl.BlockSpec(memory_space=pltpu.VMEM)
    rows, hd = parts[0].shape
    return pl.pallas_call(
        functools.partial(regroup_kernel, body=body),
        in_specs=[pl.BlockSpec(memory_space=pltpu.SMEM)] + [whole] * PIECES,
        out_specs=whole,
        out_shape=jax.ShapeDtypeStruct((body + PIECES * (rows - body), hd), parts[0].dtype),
        compiler_params=pltpu.CompilerParams(vmem_limit_bytes=4 << 20),
        name="regroup",
    )(host_block, *parts)


def far_kernel(host_block, own, got, *outs, body, bit, last):
    mine = jnp.bitwise_and(jnp.right_shift(lax.axis_index("ctx"), bit), 1)
    differ = jnp.bitwise_and(jnp.right_shift(differing(host_block), bit), 1)
    held, queries = outs if last else (outs[0].at[:body, :], outs[0].at[body:, :])
    count = own.shape[0] - body

    @pl.when(differ == 0)
    def _():
        held[...] = own[:body, :]

    @pl.when(differ == 1)
    def _():
        held[...] = got[:body, :]

    queries[pl.ds(pl.multiple_of(mine * count, 16), count), :] = own[body:, :]
    queries[pl.ds(pl.multiple_of((1 - mine) * count, 16), count), :] = got[body:, :]


def far_merged(host_block, own, got, body, bit, last):
    whole = pl.BlockSpec(memory_space=pltpu.VMEM)
    rows, hd = own.shape
    sizes = [body, 2 * (rows - body)]
    sizes = sizes if last else [sum(sizes)]
    return pl.pallas_call(
        functools.partial(far_kernel, body=body, bit=bit, last=last),
        in_specs=[pl.BlockSpec(memory_space=pltpu.SMEM)] + [whole] * 2,
        out_specs=[whole] * len(sizes),
        out_shape=[jax.ShapeDtypeStruct((r, hd), own.dtype) for r in sizes],
        compiler_params=pltpu.CompilerParams(vmem_limit_bytes=4 << 20),
        name="far_merge",
    )(host_block, own, got)


def store_kernel(k_ref, v_ref, key_ref, value_ref):
    hd = k_ref.shape[1]
    table = sign_table(hd).astype(BF16)

    def store(ref):
        r = jnp.dot(ref[...], table, preferred_element_type=F32) * hd**-0.5
        ceiling = CLIP_FACTOR * jnp.sqrt(jnp.mean(r * r, axis=-1, keepdims=True))
        return jnp.clip(r, -ceiling, ceiling)

    key_ref[...] = store(k_ref).astype(BF16)
    value_ref[...] = store(v_ref).T.astype(BF16)


def stored(keys, values):
    whole = pl.BlockSpec(memory_space=pltpu.VMEM)
    return pl.pallas_call(
        store_kernel,
        in_specs=[whole] * 2,
        out_specs=[whole] * 2,
        out_shape=[
            jax.ShapeDtypeStruct(keys.shape, BF16),
            jax.ShapeDtypeStruct(values.shape[::-1], BF16),
        ],
        compiler_params=pltpu.CompilerParams(vmem_limit_bytes=8 << 20),
        name="rotate_store",
    )(keys, values)


def partial_kernel(host_block, lens, q_ref, key_ref, value_ref, *refs, per, step):
    outs, turned = refs[:-1], refs[-1]
    me = lax.axis_index("ctx")
    spot = jnp.bitwise_and(jnp.right_shift(me, 1), SPREAD - 1)
    own_len = lens[host_block[me]]
    rows, hd = key_ref.shape
    scale = hd**-0.5
    hosts = host_block.shape[0]
    turned[...] = (
        jnp.dot(q_ref[...], sign_table(hd).astype(BF16), preferred_element_type=F32) * scale
    )
    usable = lax.broadcasted_iota(jnp.int32, (rows, 1), 0) < own_len
    for k in range(SPREAD):
        first = jnp.bitwise_xor(spot, k) * (per * step)
        rot = []
        for e in range(per):
            for c in range(hosts):
                at = pl.multiple_of(first + (c * SPREAD * per + e) * step, step)
                rot.append(turned[pl.ds(at, step), :])
        rot = jnp.concatenate(rot, axis=0).astype(BF16)
        s = lax.dot_general(key_ref[...], rot, NT, preferred_element_type=F32) * scale
        s = jnp.where(usable, s, NEG)
        m = jnp.max(s, axis=0, keepdims=True)
        p = jnp.exp(s - m)
        total = jnp.sum(p, axis=0, keepdims=True)
        outs[k][:hd, :] = jnp.dot(value_ref[...], p.astype(BF16), preferred_element_type=F32)
        outs[k][hd : hd + 1, :] = m
        outs[k][hd + 1 : hd + 2, :] = total
        outs[k][hd + 2 :, :] = jnp.zeros((TAIL - 2, rot.shape[0]), F32)


def host_partials(host_block, lens, queries, key_store, value_store, heads, step):
    hd = key_store.shape[1]
    rows = queries.shape[0]
    shape = jax.ShapeDtypeStruct((hd + TAIL, rows // SPREAD), F32)
    whole = pl.BlockSpec(memory_space=pltpu.VMEM)
    return pl.pallas_call(
        functools.partial(partial_kernel, per=heads // SPREAD, step=step),
        in_specs=[pl.BlockSpec(memory_space=pltpu.SMEM)] * 2 + [whole] * 3,
        out_specs=[whole] * SPREAD,
        out_shape=[shape] * SPREAD,
        scratch_shapes=[pltpu.VMEM((rows, hd), F32)],
        compiler_params=pltpu.CompilerParams(vmem_limit_bytes=16 << 20),
        name="host_partials",
    )(host_block, lens, queries, key_store, value_store)


def merge_values(parts, hd):
    maxima = [p[hd : hd + 1, :] for p in parts]
    overall = functools.reduce(jnp.maximum, maxima)
    factors = [jnp.exp(m - overall) for m in maxima]
    out = sum(p[:hd, :] * f for p, f in zip(parts, factors))
    total = sum(p[hd + 1 : hd + 2, :] * f for p, f in zip(parts, factors))
    return overall, total, out


def merge_kernel(*refs, hd):
    o_ref = refs[-1]
    overall, total, out = merge_values(refs[:-1], hd)
    o_ref[:hd, :] = out
    o_ref[hd : hd + 1, :] = overall
    o_ref[hd + 1 : hd + 2, :] = total
    o_ref[hd + 2 :, :] = jnp.zeros((TAIL - 2, out.shape[1]), F32)


def merged(parts, hd):
    whole = pl.BlockSpec(memory_space=pltpu.VMEM)
    return pl.pallas_call(
        functools.partial(merge_kernel, hd=hd),
        in_specs=[whole] * len(parts),
        out_specs=whole,
        out_shape=jax.ShapeDtypeStruct(parts[0].shape, F32),
        compiler_params=pltpu.CompilerParams(vmem_limit_bytes=4 << 20),
        name="merge_partials",
    )(*parts)


def finish_kernel(*refs, hd, tokens):
    o_ref = refs[-1]
    _, total, out = merge_values(refs[:-1], hd)
    turned = jnp.dot(
        sign_table(hd),
        out / total,
        preferred_element_type=F32,
        precision=lax.Precision.HIGHEST,
    )
    turned = (turned * hd**-0.5).T
    for e in range(turned.shape[0] // tokens):
        o_ref[:, e * hd : (e + 1) * hd] = turned[e * tokens : (e + 1) * tokens].astype(BF16)


def finished(parts, hd, tokens):
    whole = pl.BlockSpec(memory_space=pltpu.VMEM)
    per = parts[0].shape[1] // tokens
    return pl.pallas_call(
        functools.partial(finish_kernel, hd=hd, tokens=tokens),
        in_specs=[whole] * len(parts),
        out_specs=whole,
        out_shape=jax.ShapeDtypeStruct((tokens, per * hd), BF16),
        compiler_params=pltpu.CompilerParams(vmem_limit_bytes=4 << 20),
        name="finish_queries",
    )(*parts)


def project_kernel(*refs, groups):
    a_refs, w_ref, outs, total = refs[:SPREAD], refs[SPREAD], refs[SPREAD + 1 : -1], refs[-1]
    spot = jnp.bitwise_and(jnp.right_shift(lax.axis_index("ctx"), 1), SPREAD - 1)
    head = lax.axis_index("head")
    depth = a_refs[0].shape[1]
    acc = 0.0
    for k in range(SPREAD):
        at = pl.multiple_of(jnp.bitwise_xor(spot, k) * depth, depth)
        acc = acc + jnp.dot(a_refs[k][...], w_ref[pl.ds(at, depth), :], preferred_element_type=F32)
    total[...] = acc
    rows = total.shape[0] // groups
    for k in range(groups):
        at = pl.multiple_of(jnp.bitwise_xor(head, k) * rows, rows)
        outs[k][...] = total[pl.ds(at, rows), :]


def projected(chunks, weight, groups):
    tokens = chunks[0].shape[0]
    columns = weight.shape[1]
    whole = pl.BlockSpec(memory_space=pltpu.VMEM)
    return pl.pallas_call(
        functools.partial(project_kernel, groups=groups),
        in_specs=[whole] * (SPREAD + 1),
        out_specs=[whole] * groups,
        out_shape=[jax.ShapeDtypeStruct((tokens // groups, columns), F32)] * groups,
        scratch_shapes=[pltpu.VMEM((tokens, columns), F32)],
        compiler_params=pltpu.CompilerParams(vmem_limit_bytes=8 << 20),
        name="project",
    )(*chunks, weight)


def swap(x, axis, flip):
    size = lax.axis_size(axis)
    return lax.ppermute(x, axis, [(i, i ^ flip) for i in range(size)])


def per_device(
    ctx_queries, ctx_keys, ctx_values, new_queries, out_weight, host_block, block_lengths
):
    hosts = lax.axis_size("ctx")
    groups = lax.axis_size("head")
    bits = hosts.bit_length() - 1
    other_bits = [b for b in range(bits) if b not in SPREAD_BITS]
    heads = ctx_queries.shape[1] // HD
    tokens = new_queries.shape[0] * hosts
    body = 2 * ctx_keys.shape[0] // PIECES

    deal = list(dealt(ctx_keys, ctx_values, new_queries))
    key_store, value_store = stored(ctx_keys, ctx_values)
    deal = [deal[0]] + [swap(deal[k], "ctx", k) for k in range(1, PIECES)]
    deal[0], key_store = lax.optimization_barrier((deal[0], key_store))
    message = regrouped(host_block, deal, body)
    for b in range(2, bits):
        message = far_merged(host_block, message, swap(message, "ctx", 1 << b), body, b, b == bits - 1)
        message = message if b == bits - 1 else message[0]
    held, all_queries = message
    anchors = [held] + [swap(held, "ctx", k) for k in range(1, PIECES)]

    partials = host_partials(
        host_block, block_lengths, all_queries, key_store, value_store, heads, new_queries.shape[0]
    )
    parts = [partials[0]] + [swap(partials[k], "ctx", k << 1) for k in range(1, SPREAD)]
    one = merged(parts, HD)
    for b in other_bits[1:]:
        one = merged([one, swap(one, "ctx", 1 << b)], HD)
    other = swap(one, "ctx", 1)

    def attend(anchors, first, count, into):
        return context_attention(
            host_block, block_lengths, ctx_queries, ctx_keys, ctx_values, anchors, first, count, into
        )

    half = heads // 2
    chunk = finished([one, other], HD, tokens)
    chunks = [chunk] + [swap(chunk, "ctx", k << 1) for k in range(1, SPREAD)]
    anchors[0], _ = lax.optimization_barrier((anchors[0], chunk))
    context_out = attend(anchors, 0, half, None)
    chunks[0], context_out = lax.optimization_barrier((chunks[0], context_out))
    sums = projected(chunks, out_weight, groups)
    anchors[0], _ = lax.optimization_barrier((anchors[0], sums[0]))
    context_out = attend(anchors, half, half, context_out)
    answer = sums[0]
    for k in range(1, groups):
        answer = answer + swap(sums[k], "head", k)
    answer = answer.astype(BF16)
    return (context_out, answer)


def solution(mesh):
    placed = (
        P("ctx", "head"),
        P("ctx", "head"),
        P("ctx", "head"),
        P("ctx", "head"),
        P("head", "ctx"),
        P(),
        P(),
    )
    return jax.shard_map(
        per_device,
        mesh=mesh,
        in_specs=placed,
        out_specs=(P("ctx", "head"), P("head", "ctx")),
        check_vma=False,
    )
```
